256 devices in a mesh: section: 8 (over x, core), ctx: 32 (over z, y).
Axes of the slice: x: 4, y: 4, z: 8, core: 2. Of those that a mesh axis runs over, the one named last changes fastest.
Arguments:
- section_input: bfloat16 [8, 4096, 8192], P('section', 'ctx'), may hold values from -6 to 6
- norm_gain: bfloat16 [8, 8192], P('section'), may hold values from 0.099609375 to 1.8984375
- conv_weight: bfloat16 [8, 4, 8192], P('section'), may hold values from -3 to 3
- state_write: bfloat16 [8, 4096, 1024], P('section', 'ctx'), may hold values from -6 to 6
- state_read: bfloat16 [8, 4096, 1024], P('section', 'ctx'), may hold values from -6 to 6
- step_size: float32 [8, 128, 4096], P('section', None, 'ctx'), as said below
- log_decay: float32 [8, 128, 4096], P('section', None, 'ctx'), may hold values from -1 to 0, as said below
- skip_gain: float32 [8, 128], P('section'), may hold values from 0.1 to 1.9
Outputs:
- handed: bfloat16 [8, 4096, 8192], P('section', 'ctx')
The draws below stay inside these ranges and needn't reach their ends.
Inputs may be any that keep to these rules, and one draw needn't show every extreme that they name: `step_size`: positive. `log_decay`: never positive.
All inputs are finite; a program needn't handle non-finite values.
Results may differ from the reference program's by a relative error of at most 0.01.
Values may be sent and summed in bfloat16 or wider, within the bound.
A program may use at most 320 MiB of HBM per device.

```python
import math
import jax
import jax.numpy as jnp
from jax import lax

HEADS = 128
HEAD_DIM = 64
STATE = 128
GROUPS = 8
CONV = 4
SPAN = 128
TOK_DEV = 128
LAYERS = 8
CONTEXT_EXTENT = 4096
WIDTH = 8192


def draw_step_size(key, part):
    key = jax.random.fold_in(key, 12)
    tensor_extents = (LAYERS, HEADS, CONTEXT_EXTENT)
    norm_scale = 1.0 / math.sqrt(STATE * CONTEXT_EXTENT)
    values = jnp.exp(jax.random.uniform(key, tensor_extents, jnp.float32, math.log(0.5), math.log(2.0)))
    return values * norm_scale


def draw_log_decay(key, part):
    key = jax.random.fold_in(key, 11)
    stochastic_seeds = jax.random.split(key, 7)
    tensor_extents = (LAYERS, HEADS, CONTEXT_EXTENT)
    head_shape = (LAYERS, HEADS, 1)
    fast_share = 0.5
    picked = jax.random.uniform(stochastic_seeds[0], head_shape, jnp.float32) < fast_share
    fast_rate = jnp.exp(jax.random.uniform(stochastic_seeds[1], head_shape, jnp.float32, math.log(1.0 / 50.0), math.log(1.0 / 25.0)))
    slow_rate = jnp.exp(jax.random.uniform(stochastic_seeds[2], head_shape, jnp.float32, math.log(0.05), math.log(0.3))) / CONTEXT_EXTENT
    fading_pace = jnp.where(picked, fast_rate, slow_rate)
    symbol_coefficient = jnp.exp(jax.random.uniform(stochastic_seeds[3], tensor_extents, jnp.float32, -math.log(2.0), math.log(2.0)))
    reach_coefficient = jnp.exp(jax.random.uniform(stochastic_seeds[4], (LAYERS, HEADS, CONTEXT_EXTENT // TOK_DEV, 1), jnp.float32, -math.log(2.0), math.log(2.0)))
    reach_coefficient = jnp.broadcast_to(reach_coefficient, (LAYERS, HEADS, CONTEXT_EXTENT // TOK_DEV, TOK_DEV)).reshape(tensor_extents)
    cluster_symbols = jax.random.uniform(stochastic_seeds[5], tensor_extents, jnp.float32) < 4.0 / CONTEXT_EXTENT
    omitted_lines = jnp.exp(jax.random.uniform(stochastic_seeds[6], tensor_extents, jnp.float32, math.log(0.22), math.log(0.69)))
    return -(fading_pace * symbol_coefficient * reach_coefficient + jnp.where(cluster_symbols, omitted_lines, 0.0))


def level_of(rng, extent, cuts, smallest, top_value):
    level, own = 1.0, jax.random.fold_in(rng, 6)
    for axis_at, shards_of in cuts:
        draws = jnp.exp(jax.random.uniform(jax.random.fold_in(own, axis_at), (shards_of,), jnp.float32, smallest / len(cuts), top_value / len(cuts)))
        level = level * jnp.repeat(draws, extent[axis_at] // shards_of).reshape([-1 if axis == axis_at else 1 for axis in range(len(extent))])
    return level


def scatter_about(own_key, extent, scale, bound, pieces=(), dtype=jnp.bfloat16):
    drawn = scale * jax.random.normal(own_key, extent, jnp.float32)
    if pieces:
        drawn = drawn * level_of(own_key, extent, pieces, -0.22, 0.18)
    return jnp.clip(drawn, -bound, bound).astype(dtype)


def setup_inputs(seed: int = 0) -> dict:
    arg_keys = jax.random.split(jax.random.key(seed), 9)
    return {
        "section_input": scatter_about(arg_keys[0], (LAYERS, CONTEXT_EXTENT, WIDTH), 1.0, 6.0, ((0, 8), (1, 32))),
        "norm_gain": jnp.clip(1.0 + 0.18 * jax.random.normal(arg_keys[1], (LAYERS, WIDTH), jnp.float32), 0.099609375, 1.8984375).astype(jnp.bfloat16),
        "conv_weight": scatter_about(arg_keys[2], (LAYERS, CONV, WIDTH), CONV ** -0.5, 3.0, ((0, 8),)),
        "state_write": scatter_about(arg_keys[3], (LAYERS, CONTEXT_EXTENT, GROUPS * STATE), 1.0, 6.0, ((0, 8), (1, 32))),
        "state_read": scatter_about(arg_keys[4], (LAYERS, CONTEXT_EXTENT, GROUPS * STATE), 1.0, 6.0, ((0, 8), (1, 32))),
        "step_size": draw_step_size(jax.random.fold_in(arg_keys[8], 71), 0),
        "log_decay": draw_log_decay(jax.random.fold_in(arg_keys[8], 71), 0),
        "skip_gain": jnp.clip(1.0 + 0.18 * jax.random.normal(arg_keys[7], (LAYERS, HEADS), jnp.float32), 0.1, 1.9),
    }


def block_parts(mixed, writes, reads, steps, decays):
    per_group = HEADS // GROUPS
    cumul = jnp.cumsum(decays, axis=-1)
    scores = jnp.einsum('tgn,sgn->gts', reads.astype(jnp.float32), writes.astype(jnp.float32))
    scores = jnp.repeat(scores, per_group, axis=0)
    spread = cumul[:, :, None] - cumul[:, None, :]
    lower = jnp.arange(SPAN)[:, None] >= jnp.arange(SPAN)[None, :]
    weights = jnp.where(lower[None], scores * jnp.exp(jnp.minimum(spread, 0.0)) * steps[:, None, :], 0.0).astype(jnp.bfloat16)
    inner = jnp.einsum('hts,shp->thp', weights.astype(jnp.float32), mixed.astype(jnp.float32))
    to_end = jnp.exp(cumul[:, -1:] - cumul) * steps
    scaled = (mixed.astype(jnp.float32) * jnp.transpose(to_end)[:, :, None]).astype(jnp.bfloat16)
    scaled = scaled.reshape(SPAN, GROUPS, per_group, HEAD_DIM)
    summary = jnp.einsum('sgn,sgkp->gknp', writes.astype(jnp.float32), scaled.astype(jnp.float32))
    summary = summary.reshape(HEADS, STATE, HEAD_DIM)
    return (inner, jnp.exp(cumul[:, -1]), summary, cumul)

def carried_term(reads, cumul, entering):
    grouped = entering.reshape(GROUPS, HEADS // GROUPS, STATE, HEAD_DIM)
    term = jnp.einsum('tgn,gknp->tgkp', reads.astype(jnp.float32), grouped.astype(jnp.float32))
    term = term.reshape(SPAN, HEADS, HEAD_DIM)
    return term * jnp.transpose(jnp.exp(cumul))[:, :, None]

def layer_apply(stream, gain, conv_taps, writes, reads, steps, decays, skip):
    wide = stream.astype(jnp.float32)
    normed = (wide * lax.rsqrt(lax.optimization_barrier(jnp.mean(wide * wide, axis=-1, keepdims=True)) + 1e-05) * gain.astype(jnp.float32)).astype(jnp.bfloat16)
    padded = jnp.concatenate([jnp.zeros((CONV - 1, normed.shape[1]), jnp.bfloat16), normed], axis=0)
    total = jnp.zeros(normed.shape, jnp.float32)
    for offset in range(CONV):
        total = total + conv_taps[offset].astype(jnp.float32) * padded[offset:offset + CONTEXT_EXTENT].astype(jnp.float32)
    mixed = jax.nn.silu(total).astype(jnp.bfloat16)
    count = CONTEXT_EXTENT // SPAN
    mixed_blocks = mixed.reshape(count, SPAN, HEADS, HEAD_DIM)
    write_blocks = writes.reshape(count, SPAN, GROUPS, STATE)
    read_blocks = reads.reshape(count, SPAN, GROUPS, STATE)
    step_blocks = jnp.transpose(steps.reshape(HEADS, count, SPAN), (1, 0, 2))
    decay_blocks = jnp.transpose(decays.reshape(HEADS, count, SPAN), (1, 0, 2))

    def advance(state, items):
        mixed_part, write_part, read_part, step_part, decay_part = items
        inner, factor, summary, cumul = block_parts(mixed_part, write_part, read_part, step_part, decay_part)
        carried = carried_term(read_part, cumul, state.astype(jnp.bfloat16))
        skipped = skip[None, :, None] * mixed_part.astype(jnp.float32)
        return (factor[:, None, None] * state + summary, inner + carried + skipped)
    start = jnp.zeros((HEADS, STATE, HEAD_DIM), jnp.float32)
    _, results = lax.scan(advance, start, (mixed_blocks, write_blocks, read_blocks, step_blocks, decay_blocks))
    return (wide + results.reshape(CONTEXT_EXTENT, HEADS * HEAD_DIM)).astype(jnp.bfloat16)

def reference(section_input, norm_gain, conv_weight, state_write, state_read, step_size, log_decay, skip_gain):
    saved = []
    for layer_index in range(LAYERS):
        saved.append(layer_apply(section_input[layer_index], norm_gain[layer_index], conv_weight[layer_index], state_write[layer_index], state_read[layer_index], step_size[layer_index], log_decay[layer_index], skip_gain[layer_index]))
    outputs = jnp.stack(saved)
    return jnp.concatenate([outputs[LAYERS - 1:], outputs[:LAYERS - 1]], axis=0)
```

```python
import jax
import jax.numpy as jnp
from jax import lax
from jax.experimental import pallas as pl
from jax.experimental.pallas import tpu as pltpu
from jax.sharding import PartitionSpec as P

HEADS = 128
HEAD_DIM = 64
STATE = 128
GROUPS = 8
CONV = 4
SPAN = 128
WIDTH = HEADS * HEAD_DIM
RING = 4
LANES = 256
PAIRS = LANES // 128
CHUNK_HEADS = LANES // HEAD_DIM
CHUNKS = WIDTH // RING // LANES
GROUP_CHUNKS = WIDTH // GROUPS // LANES
LOG2E = 1.4426950408889634
F32 = jnp.float32
BF16 = jnp.bfloat16


def mixing_kernel(
    x_ref, gain_ref, taps_ref, write_ref, read_ref, step_ref, decay_ref, skip_ref,
    out_ref,
    padded, mixed, total, grown, scores, write_t, cum_cols, shift_rows, shift_cols, scale,
    halo_out, halo_in, end_out, end_in, sum_out, sum_in, state_in, state_out,
    back_out, back_in, last_out,
    halo_sem, end_sems, sum_sems, state_sems, back_sems, last_sems,
):
    sections, blocks = lax.axis_size("section"), lax.axis_size("ctx")
    rows = blocks // RING
    section, ctx = lax.axis_index("section"), lax.axis_index("ctx")
    row, place = ctx // RING, ctx % RING

    def at_ctx(index):
        return {"section": section, "ctx": index}

    def at_place(index):
        return at_ctx(row * RING + index)

    before_ctx, after_ctx = (ctx + blocks - 1) % blocks, (ctx + 1) % blocks
    before_section = {"section": (section + sections - 1) % sections, "ctx": ctx}
    after_section = {"section": (section + 1) % sections, "ctx": ctx}

    barrier = pltpu.get_barrier_semaphore()
    pl.semaphore_signal(barrier, 1, device_id=at_ctx(before_ctx))
    pl.semaphore_signal(barrier, 1, device_id=before_section)
    for distance in range(1, RING):
        pl.semaphore_signal(barrier, 1, device_id=at_place((place + distance) % RING))

    @pl.when(row > 0)
    def _():
        pl.semaphore_signal(barrier, 1, device_id=at_ctx(ctx - RING))

    def halo_copy():
        return pltpu.make_async_remote_copy(
            src_ref=halo_out, dst_ref=halo_in, send_sem=halo_sem.at[0], recv_sem=halo_sem.at[1],
            device_id=at_ctx(after_ctx),
        )

    def end_copy(to, slot):
        return pltpu.make_async_remote_copy(
            src_ref=end_out.at[to], dst_ref=end_in.at[slot],
            send_sem=end_sems.at[0, to], recv_sem=end_sems.at[1, slot], device_id=at_place(to),
        )

    def sum_copy(to, slot, j):
        return pltpu.make_async_remote_copy(
            src_ref=sum_out.at[to, j], dst_ref=sum_in.at[slot, j],
            send_sem=sum_sems.at[0, to, j], recv_sem=sum_sems.at[1, slot, j],
            device_id=at_place(to),
        )

    def state_copy(j):
        return pltpu.make_async_remote_copy(
            src_ref=state_out.at[j], dst_ref=state_in.at[j],
            send_sem=state_sems.at[0, j], recv_sem=state_sems.at[1, j],
            device_id=at_ctx((ctx + RING) % blocks),
        )

    def back_copy(to, slot, j):
        return pltpu.make_async_remote_copy(
            src_ref=back_out.at[to, j], dst_ref=back_in.at[slot, j],
            send_sem=back_sems.at[0, to, j], recv_sem=back_sems.at[1, slot, j],
            device_id=at_place(to),
        )

    def lanes_of(chunk):
        return pl.ds(pl.multiple_of(chunk * LANES, LANES), LANES)

    def last_copy(chunk):
        return pltpu.make_async_remote_copy(
            src_ref=last_out.at[chunk], dst_ref=out_ref.at[:, lanes_of(chunk)],
            send_sem=last_sems.at[0, chunk], recv_sem=last_sems.at[1, chunk],
            device_id=after_section,
        )

    def square_sum(first, count):
        def add(i, acc):
            part = x_ref[pl.ds(first, count), pl.ds(pl.multiple_of(i * 512, 512), 512)].astype(F32)
            part = part * part
            return acc + (
                (part[:, 0:128] + part[:, 128:256]) + (part[:, 256:384] + part[:, 384:512])
            )

        acc = lax.fori_loop(0, WIDTH // 512, add, jnp.zeros((count, 128), F32))
        mean = jnp.sum(acc, axis=-1, keepdims=True) * (1.0 / WIDTH)
        return jnp.broadcast_to(lax.rsqrt(mean + 1e-05), (count, 128))

    tail_scale = square_sum(SPAN - 16, 16)
    for i in range(8):
        span = slice(i * 1024, (i + 1) * 1024)
        wide = x_ref[SPAN - 16 : SPAN, span].astype(F32)
        normed = (wide * jnp.tile(tail_scale, (1, 8))) * gain_ref[:, span].astype(F32)
        normed = normed.astype(BF16).astype(F32)
        halo_out[3 * i : 3 * i + 3, :] = normed[13:16, :]

    pl.semaphore_wait(barrier, 1 + RING + jnp.where(row < rows - 1, 1, 0))

    halo_copy().start()

    token = lax.broadcasted_iota(jnp.int32, (SPAN, SPAN), 0)
    lane = lax.broadcasted_iota(jnp.int32, (SPAN, SPAN), 1)
    upper = jnp.where(token <= lane, 1.0, 0.0).astype(F32)
    cumul = lax.dot_general(
        decay_ref[...], upper, (((1,), (0,)), ((), ())),
        precision=lax.Precision.HIGHEST, preferred_element_type=F32,
    ) * LOG2E
    shift = cumul - jnp.log2(step_ref[...])
    shift_rows[...] = shift
    shift_cols[...] = shift.T
    cum_cols[...] = cumul.T
    low = lane < HEAD_DIM
    causal = token >= lane

    def columns(ref, chunk):
        return pltpu.roll(ref[...], (HEADS - chunk * CHUNK_HEADS) % HEADS, 1)

    def pair_of(cols, p):
        return jnp.where(
            low[: cols.shape[0]], cols[:, 2 * p : 2 * p + 1], cols[:, 2 * p + 1 : 2 * p + 2]
        )

    def put_ends(chunk, carry):
        cols = pltpu.roll(
            cum_cols[SPAN - 8 : SPAN, :], (HEADS - chunk * CHUNK_HEADS) % HEADS, 1
        )
        for p in range(PAIRS):
            pair = (chunk % CHUNKS) * PAIRS + p
            end_out[chunk // CHUNKS, pl.ds(pair, 1), :] = pair_of(cols, p)[7:8, :]
        return carry

    lax.fori_loop(0, RING * CHUNKS, put_ends, 0)
    for distance in range(1, RING):
        to = (place + distance) % RING
        end_copy(to, place).start()
    end_in[place] = end_out[place]

    scale[...] = square_sum(0, SPAN)

    def convolve(lanes, first, count):
        taps = taps_ref[:, lanes].astype(F32)
        acc = jnp.zeros((count, LANES), F32)
        for k in range(CONV):
            acc = acc + taps[k : k + 1, :] * padded[pl.ds(8 - (CONV - 1) + first + k, count), lanes]
        acc = acc * (0.5 + 0.5 * jnp.tanh(0.5 * acc))
        mixed[pl.ds(first, count), lanes] = acc.astype(BF16)

    def norm_chunk(i, carry):
        lanes = lanes_of(i)
        wide = x_ref[:, lanes].astype(F32)
        normed = (wide * jnp.tile(scale[...], (1, PAIRS))) * gain_ref[:, lanes].astype(F32)
        padded[pl.ds(8, SPAN), lanes] = normed.astype(BF16).astype(F32)
        convolve(lanes, 16, SPAN - 16)
        return carry

    lax.fori_loop(0, WIDTH // LANES, norm_chunk, 0)

    for g in range(GROUPS):
        span = slice(g * STATE, (g + 1) * STATE)
        writes = write_ref[:, span]
        scores[g] = lax.dot_general(
            read_ref[:, span], writes, (((1,), (1,)), ((), ())), preferred_element_type=F32
        )
        write_t[g] = writes.astype(F32).T.astype(BF16)

    halo_copy().wait()
    for i in range(8):
        rows3 = halo_in[3 * i : 3 * i + 3, :]
        padded[8 - (CONV - 1) : 8, i * 1024 : (i + 1) * 1024] = jnp.where(ctx > 0, rows3, 0.0)

    def first_rows(i, carry):
        convolve(lanes_of(i), 0, 16)
        return carry

    lax.fori_loop(0, WIDTH // LANES, first_rows, 0)

    def summarize(j, carry):
        def quarter(q, carry):
            chunk = q * CHUNKS + j
            lanes = lanes_of(chunk)
            cols = columns(shift_cols, chunk)
            parts = []
            for p in range(PAIRS):
                end = end_out[q, pl.ds(j * PAIRS + p, 1), :]
                parts.append(jnp.exp2(end - pair_of(cols, p)))
            scaled = (mixed[:, lanes].astype(F32) * jnp.concatenate(parts, axis=1)).astype(BF16)
            summary = jnp.dot(
                write_t[chunk // GROUP_CHUNKS], scaled, preferred_element_type=F32
            ).astype(BF16)
            sum_out[q, j] = summary

            @pl.when(q != place)
            def _():
                sum_copy(q, place, j).start()

            @pl.when(q == place)
            def _():
                sum_in[q, j] = summary

            return carry

        return lax.fori_loop(0, RING, quarter, carry)

    lax.fori_loop(0, CHUNKS, summarize, 0)

    for distance in range(1, RING):
        source = (place + distance) % RING
        end_copy(source, place).wait_send()
        end_copy(source, source).wait_recv()

    @pl.when(row == 0)
    def _():
        state_in[...] = jnp.zeros_like(state_in)

    def factor(source, j):
        return jnp.concatenate(
            [
                jnp.exp2(end_in[source, pl.ds(j * PAIRS + p, 1), :])
                for p in range(PAIRS)
            ],
            axis=1,
        )

    def relay(j):
        for distance in range(1, RING):
            source = (place + distance) % RING
            sum_copy(source, source, j).wait_recv()
        whole = factor(0, j)
        summed = sum_in[0, j].astype(F32)
        for block in range(1, RING):
            one = factor(block, j)
            whole = whole * one
            summed = summed * one + sum_in[block, j].astype(F32)

        @pl.when(row > 0)
        def _():
            state_copy(j).wait_recv()

        @pl.when(row < rows - 1)
        def _():
            entering = state_in[j].astype(F32)
            state_out[j] = (entering * whole + summed).astype(BF16)
            state_copy(j).start()

    def hand_back(j):
        state = state_in[j].astype(F32)
        back_out[0, j] = state_in[j]
        for block in range(1, RING):
            state = state * factor(block - 1, j) + sum_in[block - 1, j].astype(F32)
            back_out[block, j] = state.astype(BF16)
        for distance in range(1, RING):
            to = (place + distance) % RING
            back_copy(to, place, j).start()
        back_in[place, j] = back_out[place, j]

    def within(chunk, carry):
        lanes = lanes_of(chunk)
        score = scores[chunk // GROUP_CHUNKS]
        cols = columns(cum_cols, chunk)
        for p in range(PAIRS):
            at = pl.ds(pl.multiple_of(chunk * LANES + p * 128, 128), 128)
            weights = []
            spread = []
            for k in range(2):
                head = chunk * CHUNK_HEADS + 2 * p + k
                decay = jnp.broadcast_to(cols[:, 2 * p + k : 2 * p + k + 1], (SPAN, SPAN))
                spread.append(decay)
                weight = score * jnp.exp2(decay - shift_rows[pl.ds(head, 1), :])
                weights.append(jnp.where(causal, weight, 0.0).astype(BF16))
            both = mixed[:, at]
            nothing = jnp.zeros_like(both)
            apart = jnp.concatenate(
                [jnp.where(low, both, nothing), jnp.where(low, nothing, both)], axis=0
            )
            inner = jnp.dot(
                jnp.concatenate(weights, axis=1), apart, preferred_element_type=F32
            )
            head = chunk * CHUNK_HEADS + 2 * p
            skip = jnp.where(low[:1], skip_ref[0, head], skip_ref[0, head + 1])
            total[:, at] = x_ref[:, at].astype(F32) + inner + skip * both.astype(F32)
            grown[:, at] = jnp.exp2(jnp.where(low, spread[0], spread[1]))
        return carry

    def finish(j):
        for distance in range(1, RING):
            source = (place + distance) % RING
            back_copy(source, source, j).wait_recv()

        def quarter(q, carry):
            chunk = q * CHUNKS + j
            lanes = lanes_of(chunk)
            group = pl.ds(pl.multiple_of((chunk // GROUP_CHUNKS) * STATE, STATE), STATE)
            carried = jnp.dot(read_ref[:, group], back_in[q, j], preferred_element_type=F32)
            last_out[chunk] = (total[:, lanes] + grown[:, lanes] * carried).astype(BF16)
            last_copy(chunk).start()
            return carry

        lax.fori_loop(0, RING, quarter, 0)

    lag = jnp.maximum(rows - 1 - row, 0)
    ahead = jnp.minimum(row * 8, RING * CHUNKS)
    lax.fori_loop(0, ahead, within, 0)

    def pipeline(i, carry):
        @pl.when(i < CHUNKS)
        def _():
            relay(i)

        j = i - lag

        @pl.when((j >= 0) & (j < CHUNKS))
        def _():
            hand_back(j)

        return carry

    lax.fori_loop(0, lag, pipeline, 0)
    lax.fori_loop(ahead, RING * CHUNKS, within, 0)

    def pipeline_end(i, carry):
        pipeline(i, carry)
        j = i - lag - 1

        @pl.when(j >= 0)
        def _():
            finish(j)

        return carry

    lax.fori_loop(lag, lag + CHUNKS + 1, pipeline_end, 0)

    def settle(j, carry):
        for distance in range(1, RING):
            to = (place + distance) % RING
            sum_copy(to, place, j).wait_send()
            back_copy(to, place, j).wait_send()

        @pl.when(row < rows - 1)
        def _():
            state_copy(j).wait_send()

        for q in range(RING):
            last_copy(q * CHUNKS + j).wait()
        return carry

    lax.fori_loop(0, CHUNKS, settle, 0)


def shards(
    section_input, norm_gain, conv_weight, state_write, state_read, step_size, log_decay, skip_gain
):
    vmem = pl.BlockSpec(memory_space=pltpu.VMEM)
    dma = pltpu.SemaphoreType.DMA
    chunks = WIDTH // LANES
    half = (RING, CHUNKS, STATE, LANES)
    handed = pl.pallas_call(
        mixing_kernel,
        out_shape=jax.ShapeDtypeStruct((SPAN, WIDTH), BF16),
        in_specs=[vmem] * 7 + [pl.BlockSpec(memory_space=pltpu.SMEM)],
        out_specs=pl.BlockSpec(memory_space=pl.ANY),
        scratch_shapes=[
            pltpu.VMEM((SPAN + 8, WIDTH), F32),
            pltpu.VMEM((SPAN, WIDTH), BF16),
            pltpu.VMEM((SPAN, WIDTH), F32),
            pltpu.VMEM((SPAN, WIDTH), F32),
            pltpu.VMEM((GROUPS, SPAN, SPAN), F32),
            pltpu.VMEM((GROUPS, STATE, SPAN), BF16),
            pltpu.VMEM((SPAN, HEADS), F32),
            pltpu.VMEM((HEADS, SPAN), F32),
            pltpu.VMEM((SPAN, HEADS), F32),
            pltpu.VMEM((SPAN, 128), F32),
            pltpu.VMEM((24, 1024), F32),
            pltpu.VMEM((24, 1024), F32),
            pltpu.VMEM((RING, CHUNKS * PAIRS, 128), F32),
            pltpu.VMEM((RING, CHUNKS * PAIRS, 128), F32),
            pltpu.VMEM(half, BF16),
            pltpu.VMEM(half, BF16),
            pltpu.VMEM(half[1:], BF16),
            pltpu.VMEM(half[1:], BF16),
            pltpu.VMEM(half, BF16),
            pltpu.VMEM(half, BF16),
            pltpu.VMEM((chunks, SPAN, LANES), BF16),
            dma((2,)),
            dma((2, RING)),
            dma((2, RING, CHUNKS)),
            dma((2, CHUNKS)),
            dma((2, RING, CHUNKS)),
            dma((2, chunks)),
        ],
        compiler_params=pltpu.CompilerParams(
            collective_id=0, has_side_effects=True, vmem_limit_bytes=52 << 20
        ),
    )(
        section_input[0],
        norm_gain,
        conv_weight[0],
        state_write[0],
        state_read[0],
        step_size[0],
        log_decay[0],
        skip_gain,
    )
    return handed[None]


def solution(mesh):
    in_specs = (
        P("section", "ctx", None),
        P("section", None),
        P("section", None, None),
        P("section", "ctx", None),
        P("section", "ctx", None),
        P("section", None, "ctx"),
        P("section", None, "ctx"),
        P("section", None),
    )
    out_specs = P("section", "ctx", None)
    return jax.shard_map(shards, mesh=mesh, in_specs=in_specs, out_specs=out_specs, check_vma=False)
```

```python
import jax
import jax.numpy as jnp
from jax import lax
from jax.experimental import pallas as pl
from jax.experimental.pallas import tpu as pltpu
from jax.sharding import PartitionSpec as P

HEADS = 128
HEAD_DIM = 64
STATE = 128
GROUPS = 8
CONV = 4
SPAN = 128
WIDTH = HEADS * HEAD_DIM
RING = 4
LANES = 256
PAIRS = LANES // 128
CHUNK_HEADS = LANES // HEAD_DIM
CHUNKS = WIDTH // RING // LANES
GROUP_CHUNKS = WIDTH // GROUPS // LANES
LOG2E = 1.4426950408889634
F32 = jnp.float32
BF16 = jnp.bfloat16


def mixing_kernel(
    x_hbm, gain_hbm, taps_hbm, write_hbm, read_hbm, step_hbm, decay_hbm, skip_ref,
    out_ref,
    x_ref, gain_ref, taps_ref, write_ref, read_ref, step_ref, decay_ref,
    scale_buf, padded, mixed, total, grown, scores, write_t, cum_rows, cum_cols, shift_rows, shift_cols,
    halo_out, halo_in, end_out, end_in, sum_out, sum_in, state_in, state_out,
    back_out, back_in, last_out,
    fetch_sems, halo_sems, end_sems, sum_sems, state_sems, back_sems, last_sems,
):
    sections, blocks = lax.axis_size("section"), lax.axis_size("ctx")
    rows = blocks // RING
    section, ctx = lax.axis_index("section"), lax.axis_index("ctx")
    row, place = ctx // RING, ctx % RING

    def at_ctx(index):
        return {"section": section, "ctx": index}

    def at_place(index):
        return at_ctx(row * RING + index)

    before_ctx, after_ctx = (ctx + blocks - 1) % blocks, (ctx + 1) % blocks
    before_section = {"section": (section + sections - 1) % sections, "ctx": ctx}
    after_section = {"section": (section + 1) % sections, "ctx": ctx}

    late = SPAN - 16
    fetches = [
        pltpu.make_async_copy(source, target, fetch_sems.at[i])
        for i, (source, target) in enumerate(
            [
                (x_hbm.at[pl.ds(late, 16)], x_ref.at[pl.ds(late, 16)]),
                (gain_hbm, gain_ref),
                (decay_hbm, decay_ref),
                (step_hbm, step_ref),
                (x_hbm.at[pl.ds(0, late)], x_ref.at[pl.ds(0, late)]),
                (taps_hbm, taps_ref),
                (write_hbm, write_ref),
                (read_hbm, read_ref),
            ]
        )
    ]
    for fetch in fetches:
        fetch.start()

    barrier = pltpu.get_barrier_semaphore()
    pl.semaphore_signal(barrier, 1, device_id=before_section)
    for distance in range(1, RING):
        pl.semaphore_signal(barrier, 1, device_id=at_place((place + distance) % RING))

    @pl.when(ctx > 0)
    def _():
        pl.semaphore_signal(barrier, 1, device_id=at_ctx(before_ctx))

    @pl.when(row > 0)
    def _():
        pl.semaphore_signal(barrier, 1, device_id=at_ctx(ctx - RING))

    def halo_copy(j):
        return pltpu.make_async_remote_copy(
            src_ref=halo_out.at[j], dst_ref=halo_in.at[j],
            send_sem=halo_sems.at[0, j], recv_sem=halo_sems.at[1, j],
            device_id=at_ctx(after_ctx),
        )

    def end_copy(to, slot):
        return pltpu.make_async_remote_copy(
            src_ref=end_out.at[to], dst_ref=end_in.at[slot],
            send_sem=end_sems.at[0, to], recv_sem=end_sems.at[1, slot], device_id=at_place(to),
        )

    def sum_copy(to, slot, j):
        return pltpu.make_async_remote_copy(
            src_ref=sum_out.at[to, j], dst_ref=sum_in.at[slot, j],
            send_sem=sum_sems.at[0, to, j], recv_sem=sum_sems.at[1, slot, j],
            device_id=at_place(to),
        )

    def state_copy(j):
        return pltpu.make_async_remote_copy(
            src_ref=state_out.at[j], dst_ref=state_in.at[j],
            send_sem=state_sems.at[0, j], recv_sem=state_sems.at[1, j],
            device_id=at_ctx((ctx + RING) % blocks),
        )

    def back_copy(to, slot, j):
        return pltpu.make_async_remote_copy(
            src_ref=back_out.at[to, j], dst_ref=back_in.at[slot, j],
            send_sem=back_sems.at[0, to, j], recv_sem=back_sems.at[1, slot, j],
            device_id=at_place(to),
        )

    def lanes_of(chunk):
        return pl.ds(pl.multiple_of(chunk * LANES, LANES), LANES)

    def last_copy(chunk):
        return pltpu.make_async_remote_copy(
            src_ref=last_out.at[chunk], dst_ref=out_ref.at[:, lanes_of(chunk)],
            send_sem=last_sems.at[0, chunk], recv_sem=last_sems.at[1, chunk],
            device_id=after_section,
        )

    def square_sum(first, count):
        def add(i, acc):
            part = x_ref[pl.ds(first, count), pl.ds(pl.multiple_of(i * 1024, 1024), 1024)]
            for k in range(8):
                piece = part[:, k * 128 : (k + 1) * 128].astype(F32)
                acc = acc + piece * piece
            return acc

        acc = lax.fori_loop(0, WIDTH // 1024, add, jnp.zeros((count, 128), F32))
        mean = jnp.sum(acc, axis=-1, keepdims=True) * (1.0 / WIDTH)
        return jnp.broadcast_to(lax.rsqrt(mean + 1e-05), (count, 128))

    fetches[0].wait()
    fetches[1].wait()
    tail_scale = square_sum(late, 16)
    for chunk in range(RING * CHUNKS):
        for p in range(PAIRS):
            span = slice(chunk * LANES + p * 128, chunk * LANES + p * 128 + 128)
            normed = (x_ref[late:SPAN, span].astype(F32) * tail_scale) * gain_ref[:, span].astype(F32)
            normed = normed.astype(BF16).astype(F32)
            halo_out[chunk % CHUNKS, chunk // CHUNKS, 4 * p : 4 * p + 3, :] = normed[13:16, :]

    pl.semaphore_wait(
        barrier, RING + jnp.where(ctx < blocks - 1, 1, 0) + jnp.where(row < rows - 1, 1, 0)
    )

    @pl.when(ctx < blocks - 1)
    def _():
        for j in range(CHUNKS):
            halo_copy(j).start()

    @pl.when(ctx == 0)
    def _():
        halo_in[...] = jnp.zeros_like(halo_in)

    token = lax.broadcasted_iota(jnp.int32, (SPAN, SPAN), 0)
    lane = lax.broadcasted_iota(jnp.int32, (SPAN, SPAN), 1)
    low = lane < HEAD_DIM
    causal = token >= lane
    upper = jnp.where(token <= lane, 1.0, 0.0).astype(F32)
    fetches[2].wait()
    cumul = lax.dot_general(
        decay_ref[...], upper, (((1,), (0,)), ((), ())),
        precision=lax.Precision.HIGHEST, preferred_element_type=F32,
    ) * LOG2E
    cum_rows[...] = cumul
    even, odd = (
        jnp.broadcast_to(cum_rows[pl.ds(first, HEADS // 2, stride=2), :][:, SPAN - 1 :], (HEADS // 2, 128))
        for first in range(2)
    )
    end_out[...] = jnp.where(low[: HEADS // 2], even, odd).reshape(RING, CHUNKS * PAIRS, 128)
    for distance in range(1, RING):
        to = (place + distance) % RING
        end_copy(to, place).start()
    end_in[place] = end_out[place]
    cum_cols[...] = cumul.T
    fetches[3].wait()
    shift = cumul - jnp.log2(step_ref[...])
    shift_rows[...] = shift
    shift_cols[...] = shift.T

    fetches[4].wait()
    scale = square_sum(0, SPAN)
    for fetch in fetches[5:]:
        fetch.wait()

    for g in range(GROUPS):
        span = slice(g * STATE, (g + 1) * STATE)
        writes = write_ref[:, span]
        scores[g] = lax.dot_general(
            read_ref[:, span], writes, (((1,), (1,)), ((), ())), preferred_element_type=F32
        )
        write_t[g] = writes.astype(F32).T.astype(BF16)

    def columns(ref, j):
        return pltpu.roll(ref[...], (HEADS - j * CHUNK_HEADS) % HEADS, 1)

    def pair_lanes(chunk, p):
        return pl.ds(pl.multiple_of(chunk * LANES + p * 128, 128), 128)

    scale_buf[...] = scale

    def produce(j):
        @pl.when(ctx > 0)
        def _():
            halo_copy(j).wait_recv()

        cols = columns(shift_cols, j)
        for q in range(RING):
            chunk = q * CHUNKS + j
            parts = []
            for p in range(PAIRS):
                at = pair_lanes(chunk, p)
                buffer = padded.at[q * PAIRS + p]
                normed = (x_ref[:, at].astype(F32) * scale_buf[...]) * gain_ref[:, at].astype(F32)
                buffer[8:, :] = normed.astype(BF16).astype(F32)
                buffer[8 - (CONV - 1) : 8, :] = halo_in[j, q, 4 * p : 4 * p + 3, :]
                taps = taps_ref[:, at].astype(F32)
                acc = taps[0:1, :] * buffer[8 - (CONV - 1) : 8 - (CONV - 1) + SPAN, :]
                for k in range(1, CONV):
                    first = 8 - (CONV - 1) + k
                    acc = acc + taps[k : k + 1, :] * buffer[first : first + SPAN, :]
                acc = acc * (0.5 + 0.5 * jnp.tanh(0.5 * acc))
                value = acc.astype(BF16)
                mixed[:, at] = value
                head = q * (HEADS // RING) + 2 * p
                spread = jnp.where(low, cols[:, head : head + 1], cols[:, head + 1 : head + 2])
                end = end_out[q, pl.ds(j * PAIRS + p, 1), :]
                parts.append((value.astype(F32) * jnp.exp2(end - spread)).astype(BF16))
            sum_out[q, j] = jnp.dot(
                write_t[chunk // GROUP_CHUNKS],
                jnp.concatenate(parts, axis=1),
                preferred_element_type=F32,
            ).astype(BF16)
        for distance in (2, 1, 3):
            sum_copy((place + distance) % RING, place, j).start()
        sum_in[place, j] = sum_out[place, j]

    @pl.when(row == 0)
    def _():
        state_in[...] = jnp.zeros_like(state_in)

    def factor(source, j):
        return jnp.concatenate(
            [jnp.exp2(end_in[source, pl.ds(j * PAIRS + p, 1), :]) for p in range(PAIRS)], axis=1
        )

    def relay(j):
        for distance in range(1, RING):
            source = (place + distance) % RING
            sum_copy(source, source, j).wait_recv()
        whole = factor(0, j)
        summed = sum_in[0, j].astype(F32)
        for block in range(1, RING):
            one = factor(block, j)
            whole = whole * one
            summed = summed * one + sum_in[block, j].astype(F32)

        @pl.when(row > 0)
        def _():
            state_copy(j).wait_recv()

        @pl.when(row < rows - 1)
        def _():
            entering = state_in[j].astype(F32)
            state_out[j] = (entering * whole + summed).astype(BF16)
            state_copy(j).start()

    def hand_back(j):
        state = state_in[j].astype(F32)
        back_out[0, j] = state_in[j]
        for block in range(1, RING):
            state = state * factor(block - 1, j) + sum_in[block - 1, j].astype(F32)
            back_out[block, j] = state.astype(BF16)
        for distance in range(1, RING):
            to = (place + distance) % RING
            back_copy(to, place, j).start()
        back_in[place, j] = back_out[place, j]

    def within(j):
        cols = columns(cum_cols, j)
        for q in range(RING):
            chunk = q * CHUNKS + j
            score = scores[chunk // GROUP_CHUNKS]
            for p in range(PAIRS):
                at = pair_lanes(chunk, p)
                weights = []
                spread = []
                for k in range(2):
                    lane_at = q * (HEADS // RING) + 2 * p + k
                    decay = jnp.broadcast_to(cols[:, lane_at : lane_at + 1], (SPAN, SPAN))
                    spread.append(decay)
                    row_at = pl.ds(chunk * CHUNK_HEADS + 2 * p + k, 1)
                    weight = score * jnp.exp2(decay - shift_rows[row_at, :])
                    weights.append(jnp.where(causal, weight, 0.0).astype(BF16))
                both = mixed[:, at]
                nothing = jnp.zeros_like(both)
                apart = jnp.concatenate(
                    [jnp.where(low, both, nothing), jnp.where(low, nothing, both)], axis=0
                )
                inner = jnp.dot(
                    jnp.concatenate(weights, axis=1), apart, preferred_element_type=F32
                )
                head = chunk * CHUNK_HEADS + 2 * p
                skip = jnp.where(low[:1], skip_ref[0, head], skip_ref[0, head + 1])
                total[:, at] = x_ref[:, at].astype(F32) + inner + skip * both.astype(F32)
                grown[:, at] = jnp.exp2(jnp.where(low, spread[0], spread[1]))

    def finish(j):
        for distance in range(1, RING):
            source = (place + distance) % RING
            back_copy(source, source, j).wait_recv()
        for q in range(RING):
            chunk = q * CHUNKS + j
            lanes = lanes_of(chunk)
            group = pl.ds(pl.multiple_of((chunk // GROUP_CHUNKS) * STATE, STATE), STATE)
            carried = jnp.dot(read_ref[:, group], back_in[q, j], preferred_element_type=F32)
            last_out[chunk] = (total[:, lanes] + grown[:, lanes] * carried).astype(BF16)
        for q in range(RING):
            last_copy(q * CHUNKS + j).start()

    early = jnp.where(row == 0, 3, 0)
    begun = CHUNKS - early

    def first_steps(i, carry):
        produce(i)

        @pl.when(i == 0)
        def _():
            for distance in range(1, RING):
                source = (place + distance) % RING
                end_copy(source, place).wait_send()
                end_copy(source, source).wait_recv()

        @pl.when(i >= begun)
        def _():
            relay(i - begun)

        return carry

    lax.fori_loop(0, CHUNKS, first_steps, 0)

    def only_within(i, carry):
        within(i)
        return carry

    ahead = jnp.clip(5 * row - 4, 0, CHUNKS)
    lax.fori_loop(0, ahead, only_within, 0)
    lag = jnp.maximum(rows - 1 - row, 0)

    def last_steps(i, carry):
        @pl.when(i < CHUNKS)
        def _():
            relay(i)

        j = i - lag

        @pl.when((j >= 0) & (j < CHUNKS))
        def _():
            hand_back(j)

        piece = ahead + i - early

        @pl.when(piece < CHUNKS)
        def _():
            within(piece)

        @pl.when(j >= 1)
        def _():
            finish(j - 1)

        return carry

    lax.fori_loop(early, lag + CHUNKS + 1, last_steps, 0)

    def settle(j, carry):
        for distance in range(1, RING):
            to = (place + distance) % RING
            sum_copy(to, place, j).wait_send()
            back_copy(to, place, j).wait_send()

        @pl.when(ctx < blocks - 1)
        def _():
            halo_copy(j).wait_send()

        @pl.when(row < rows - 1)
        def _():
            state_copy(j).wait_send()

        for q in range(RING):
            last_copy(q * CHUNKS + j).wait()
        return carry

    lax.fori_loop(0, CHUNKS, settle, 0)


def shards(
    section_input, norm_gain, conv_weight, state_write, state_read, step_size, log_decay, skip_gain
):
    hbm = pl.BlockSpec(memory_space=pltpu.HBM)
    dma = pltpu.SemaphoreType.DMA
    chunks = WIDTH // LANES
    half = (RING, CHUNKS, STATE, LANES)
    halo = (CHUNKS, RING, 8, 128)
    handed = pl.pallas_call(
        mixing_kernel,
        out_shape=jax.ShapeDtypeStruct((SPAN, WIDTH), BF16),
        in_specs=[hbm] * 7 + [pl.BlockSpec(memory_space=pltpu.SMEM)],
        out_specs=pl.BlockSpec(memory_space=pltpu.VMEM),
        scratch_shapes=[
            pltpu.VMEM((SPAN, WIDTH), BF16),
            pltpu.VMEM((1, WIDTH), BF16),
            pltpu.VMEM((CONV, WIDTH), BF16),
            pltpu.VMEM((SPAN, GROUPS * STATE), BF16),
            pltpu.VMEM((SPAN, GROUPS * STATE), BF16),
            pltpu.VMEM((HEADS, SPAN), F32),
            pltpu.VMEM((HEADS, SPAN), F32),
            pltpu.VMEM((SPAN, 128), F32),
            pltpu.VMEM((RING * PAIRS, SPAN + 8, 128), F32),
            pltpu.VMEM((SPAN, WIDTH), BF16),
            pltpu.VMEM((SPAN, WIDTH), F32),
            pltpu.VMEM((SPAN, WIDTH), F32),
            pltpu.VMEM((GROUPS, SPAN, SPAN), F32),
            pltpu.VMEM((GROUPS, STATE, SPAN), BF16),
            pltpu.VMEM((HEADS, SPAN), F32),
            pltpu.VMEM((SPAN, HEADS), F32),
            pltpu.VMEM((HEADS, SPAN), F32),
            pltpu.VMEM((SPAN, HEADS), F32),
            pltpu.VMEM(halo, F32),
            pltpu.VMEM(halo, F32),
            pltpu.VMEM((RING, CHUNKS * PAIRS, 128), F32),
            pltpu.VMEM((RING, CHUNKS * PAIRS, 128), F32),
            pltpu.VMEM(half, BF16),
            pltpu.VMEM(half, BF16),
            pltpu.VMEM(half[1:], BF16),
            pltpu.VMEM(half[1:], BF16),
            pltpu.VMEM(half, BF16),
            pltpu.VMEM(half, BF16),
            pltpu.VMEM((chunks, SPAN, LANES), BF16),
            dma((8,)),
            dma((2, CHUNKS)),
            dma((2, RING)),
            dma((2, RING, CHUNKS)),
            dma((2, CHUNKS)),
            dma((2, RING, CHUNKS)),
            dma((2, chunks)),
        ],
        compiler_params=pltpu.CompilerParams(
            collective_id=0, has_side_effects=True, vmem_limit_bytes=48 << 20
        ),
    )(
        *(
            pltpu.with_memory_space_constraint(operand, pltpu.HBM)
            for operand in (
                section_input[0],
                norm_gain,
                conv_weight[0],
                state_write[0],
                state_read[0],
                step_size[0],
                log_decay[0],
            )
        ),
        skip_gain,
    )
    return handed[None]


def solution(mesh):
    in_specs = (
        P("section", "ctx", None),
        P("section", None),
        P("section", None, None),
        P("section", "ctx", None),
        P("section", "ctx", None),
        P("section", None, "ctx"),
        P("section", None, "ctx"),
        P("section", None),
    )
    out_specs = P("section", "ctx", None)
    return jax.shard_map(shards, mesh=mesh, in_specs=in_specs, out_specs=out_specs, check_vma=False)
```

```python
import jax
import jax.numpy as jnp
from jax import lax
from jax.experimental import pallas as pl
from jax.experimental.pallas import tpu as pltpu
from jax.sharding import PartitionSpec as P

HEADS = 128
HEAD_DIM = 64
STATE = 128
GROUPS = 8
CONV = 4
SPAN = 128
WIDTH = HEADS * HEAD_DIM
RING = 4
LANES = 256
PAIRS = LANES // 128
CHUNK_HEADS = LANES // HEAD_DIM
CHUNKS = WIDTH // RING // LANES
GROUP_CHUNKS = WIDTH // GROUPS // LANES
LATER = 3
EVEN = 3
ODD = 3
LAG = 5
LOG2E = 1.4426950408889634
F32 = jnp.float32
BF16 = jnp.bfloat16


def mixing_kernel(
    x_hbm, gain_hbm, taps_hbm, write_hbm, read_hbm, step_hbm, decay_hbm, skip_ref,
    out_ref,
    x_ref, gain_ref, taps_ref, write_ref, read_ref, step_ref, decay_ref,
    scale_buf, padded, mixed, grown, scores, write_t, cum_rows, cum_cols, shift_rows, shift_cols,
    halo_out, halo_in, end_out, end_in, sum_out, sum_in, state_in, state_out,
    front_out, front_in, fade_out, fade_in,
    back_out, back_in, part_out, part_in, read_in, cum_in,
    fetch_sems, halo_sems, end_sems, sum_sems, state_sems, front_sems, fade_sems, back_sems, part_sems, map_sems,
):
    sections, blocks = lax.axis_size("section"), lax.axis_size("ctx")
    rows = blocks // RING
    section, ctx = lax.axis_index("section"), lax.axis_index("ctx")
    row, place = ctx // RING, ctx % RING
    second = row % 2 == 1
    passes_on = second & (row < rows - 1)

    def at_ctx(index):
        return {"section": section, "ctx": index}

    def at_place(index):
        return at_ctx(row * RING + index)

    before_ctx, after_ctx = (ctx + blocks - 1) % blocks, (ctx + 1) % blocks
    before_section, after_section = (section + sections - 1) % sections, (section + 1) % sections

    def next_layer(index):
        return {"section": after_section, "ctx": row * RING + index}

    late = SPAN - 16
    fetches = [
        pltpu.make_async_copy(source, target, fetch_sems.at[i])
        for i, (source, target) in enumerate(
            [
                (x_hbm.at[pl.ds(late, 16)], x_ref.at[pl.ds(late, 16)]),
                (gain_hbm, gain_ref),
                (decay_hbm, decay_ref),
                (step_hbm, step_ref),
                (x_hbm.at[pl.ds(0, late)], x_ref.at[pl.ds(0, late)]),
                (taps_hbm, taps_ref),
                (write_hbm, write_ref),
                (read_hbm, read_ref),
            ]
        )
    ]
    for fetch in fetches:
        fetch.start()

    barrier = pltpu.get_barrier_semaphore()
    for index in range(RING):
        holder = {"section": before_section, "ctx": row * RING + index}
        pl.semaphore_signal(barrier, 1, device_id=holder)
    for distance in range(1, RING):
        pl.semaphore_signal(barrier, 1, device_id=at_place((place + distance) % RING))

    @pl.when(ctx > 0)
    def _():
        pl.semaphore_signal(barrier, 1, device_id=at_ctx(before_ctx))

    @pl.when(row > 0)
    def _():
        pl.semaphore_signal(barrier, 1, device_id=at_ctx(ctx - RING))

    @pl.when(second & (row > 1))
    def _():
        pl.semaphore_signal(barrier, 1, device_id=at_ctx(ctx - 2 * RING))

    def halo_copy(j):
        return pltpu.make_async_remote_copy(
            src_ref=halo_out.at[j], dst_ref=halo_in.at[j],
            send_sem=halo_sems.at[0, j], recv_sem=halo_sems.at[1, j],
            device_id=at_ctx(after_ctx),
        )

    def end_copy(to, slot):
        return pltpu.make_async_remote_copy(
            src_ref=end_out.at[to], dst_ref=end_in.at[slot],
            send_sem=end_sems.at[0, to], recv_sem=end_sems.at[1, slot], device_id=at_place(to),
        )

    def sum_copy(to, slot, j):
        return pltpu.make_async_remote_copy(
            src_ref=sum_out.at[to, j], dst_ref=sum_in.at[slot, j],
            send_sem=sum_sems.at[0, to, j], recv_sem=sum_sems.at[1, slot, j],
            device_id=at_place(to),
        )

    def state_copy(j, hops):
        return pltpu.make_async_remote_copy(
            src_ref=state_out.at[j], dst_ref=state_in.at[j],
            send_sem=state_sems.at[hops, j], recv_sem=state_sems.at[0, j],
            device_id=at_ctx((ctx + hops * RING) % blocks),
        )

    def front_copy(j):
        return pltpu.make_async_remote_copy(
            src_ref=front_out.at[j], dst_ref=front_in.at[j],
            send_sem=front_sems.at[0, j], recv_sem=front_sems.at[1, j],
            device_id=at_ctx((ctx + RING) % blocks),
        )

    def fade_copy():
        return pltpu.make_async_remote_copy(
            src_ref=fade_out, dst_ref=fade_in, send_sem=fade_sems.at[0], recv_sem=fade_sems.at[1],
            device_id=at_ctx((ctx + RING) % blocks),
        )

    def back_copy(to, slot, j):
        return pltpu.make_async_remote_copy(
            src_ref=back_out.at[to, j], dst_ref=back_in.at[slot, j],
            send_sem=back_sems.at[0, to, j], recv_sem=back_sems.at[1, slot, j],
            device_id=next_layer(to),
        )

    def lanes_of(chunk):
        return pl.ds(pl.multiple_of(chunk * LANES, LANES), LANES)

    def part_copy(chunk):
        return pltpu.make_async_remote_copy(
            src_ref=part_out.at[chunk], dst_ref=part_in.at[chunk],
            send_sem=part_sems.at[0, chunk], recv_sem=part_sems.at[1, chunk],
            device_id=next_layer(place),
        )

    def map_copies(*which):
        return [
            pltpu.make_async_remote_copy(
                src_ref=source, dst_ref=target,
                send_sem=map_sems.at[0, i], recv_sem=map_sems.at[1, i],
                device_id=next_layer(place),
            )
            for i, (source, target) in enumerate([(cum_cols, cum_in), (read_ref, read_in)])
            if i in which
        ]

    def square_sum(first, count):
        def add(i, acc):
            part = x_ref[pl.ds(first, count), pl.ds(pl.multiple_of(i * 1024, 1024), 1024)]
            for k in range(8):
                piece = part[:, k * 128 : (k + 1) * 128].astype(F32)
                acc = acc + piece * piece
            return acc

        acc = lax.fori_loop(0, WIDTH // 1024, add, jnp.zeros((count, 128), F32))
        mean = jnp.sum(acc, axis=-1, keepdims=True) * (1.0 / WIDTH)
        return jnp.broadcast_to(lax.rsqrt(mean + 1e-05), (count, 128))

    fetches[0].wait()
    fetches[1].wait()
    tail_scale = square_sum(late, 16)
    for chunk in range(RING * CHUNKS):
        for p in range(PAIRS):
            span = slice(chunk * LANES + p * 128, chunk * LANES + p * 128 + 128)
            normed = (x_ref[late:SPAN, span].astype(F32) * tail_scale) * gain_ref[:, span].astype(F32)
            normed = normed.astype(BF16).astype(F32)
            halo_out[chunk % CHUNKS, chunk // CHUNKS, 4 * p : 4 * p + 3, :] = normed[13:16, :]

    pl.semaphore_wait(
        barrier,
        2 * RING - 1
        + jnp.where(ctx < blocks - 1, 1, 0)
        + jnp.where(second, jnp.where(row < rows - 1, 2, 0), 1),
    )

    @pl.when(ctx < blocks - 1)
    def _():
        for j in range(CHUNKS):
            halo_copy(j).start()

    @pl.when(ctx == 0)
    def _():
        halo_in[...] = jnp.zeros_like(halo_in)

    token = lax.broadcasted_iota(jnp.int32, (SPAN, SPAN), 0)
    lane = lax.broadcasted_iota(jnp.int32, (SPAN, SPAN), 1)
    low = lane < HEAD_DIM
    causal = token >= lane
    upper = jnp.where(token <= lane, 1.0, 0.0).astype(F32)
    fetches[2].wait()
    cumul = lax.dot_general(
        decay_ref[...], upper, (((1,), (0,)), ((), ())),
        precision=lax.Precision.HIGHEST, preferred_element_type=F32,
    ) * LOG2E
    cum_rows[...] = cumul
    even, odd = (
        jnp.broadcast_to(cum_rows[pl.ds(first, HEADS // 2, stride=2), :][:, SPAN - 1 :], (HEADS // 2, 128))
        for first in range(2)
    )
    end_out[...] = jnp.where(low[: HEADS // 2], even, odd).reshape(RING, CHUNKS * PAIRS, 128)
    for distance in range(1, RING):
        to = (place + distance) % RING
        end_copy(to, place).start()
    end_in[place] = end_out[place]
    cum_cols[...] = cumul.T
    map_copies(0)[0].start()
    fetches[3].wait()
    shift = cumul - jnp.log2(step_ref[...])
    shift_rows[...] = shift
    shift_cols[...] = shift.T

    fetches[4].wait()
    scale = square_sum(0, SPAN)
    for fetch in fetches[5:]:
        fetch.wait()
    map_copies(1)[0].start()

    for g in range(GROUPS):
        span = slice(g * STATE, (g + 1) * STATE)
        writes = write_ref[:, span]
        scores[g] = lax.dot_general(
            read_ref[:, span], writes, (((1,), (1,)), ((), ())), preferred_element_type=F32
        )
        write_t[g] = writes.astype(F32).T.astype(BF16)

    def columns(ref, j):
        return pltpu.roll(ref[...], (HEADS - j * CHUNK_HEADS) % HEADS, 1)

    def pair_lanes(chunk, p):
        return pl.ds(pl.multiple_of(chunk * LANES + p * 128, 128), 128)

    scale_buf[...] = scale

    def produce(j):
        @pl.when(ctx > 0)
        def _():
            halo_copy(j).wait_recv()

        cols = columns(shift_cols, j)
        for q in range(RING):
            chunk = q * CHUNKS + j
            parts = []
            for p in range(PAIRS):
                at = pair_lanes(chunk, p)
                buffer = padded.at[q * PAIRS + p]
                normed = (x_ref[:, at].astype(F32) * scale_buf[...]) * gain_ref[:, at].astype(F32)
                buffer[8:, :] = normed.astype(BF16).astype(F32)
                buffer[8 - (CONV - 1) : 8, :] = halo_in[j, q, 4 * p : 4 * p + 3, :]
                taps = taps_ref[:, at].astype(F32)
                acc = taps[0:1, :] * buffer[8 - (CONV - 1) : 8 - (CONV - 1) + SPAN, :]
                for k in range(1, CONV):
                    first = 8 - (CONV - 1) + k
                    acc = acc + taps[k : k + 1, :] * buffer[first : first + SPAN, :]
                acc = acc * (0.5 + 0.5 * jnp.tanh(0.5 * acc))
                value = acc.astype(BF16)
                mixed[:, at] = value
                head = q * (HEADS // RING) + 2 * p
                spread = jnp.where(low, cols[:, head : head + 1], cols[:, head + 1 : head + 2])
                end = end_out[q, pl.ds(j * PAIRS + p, 1), :]
                parts.append((value.astype(F32) * jnp.exp2(end - spread)).astype(BF16))
            sum_out[q, j] = jnp.dot(
                write_t[chunk // GROUP_CHUNKS],
                jnp.concatenate(parts, axis=1),
                preferred_element_type=F32,
            ).astype(BF16)
        for distance in (2, 1, 3):
            sum_copy((place + distance) % RING, place, j).start()
        sum_in[place, j] = sum_out[place, j]

    @pl.when(row < 2)
    def _():
        state_in[...] = jnp.zeros_like(state_in)

    @pl.when(jnp.logical_not(second))
    def _():
        front_in[...] = jnp.zeros_like(front_in)
        fade_in[...] = jnp.zeros_like(fade_in)

    def spread_row(ref, j):
        return jnp.concatenate(
            [jnp.exp2(ref[pl.ds(j * PAIRS + p, 1), :]) for p in range(PAIRS)], axis=1
        )

    def factor(source, j):
        return spread_row(end_in.at[source], j)

    def relay(j):
        for distance in range(1, RING):
            source = (place + distance) % RING
            sum_copy(source, source, j).wait_recv()
        whole = factor(0, j)
        summed = sum_in[0, j].astype(F32)
        for block in range(1, RING):
            one = factor(block, j)
            whole = whole * one
            summed = summed * one + sum_in[block, j].astype(F32)

        @pl.when(jnp.logical_not(second))
        def _():
            front_out[j] = summed.astype(BF16)
            front_copy(j).start()

        @pl.when(second)
        def _():
            front_copy(j).wait_recv()

            @pl.when(row > 1)
            def _():
                state_copy(j, 1).wait_recv()

        @pl.when(passes_on)
        def _():
            state_out[j] = (entering(j) * whole + summed).astype(BF16)
            state_copy(j, 2).start()
            state_copy(j, 1).start()

    def entering(j):
        return state_in[j].astype(F32) * spread_row(fade_in, j) + front_in[j].astype(F32)

    def hand_back(j):
        @pl.when(jnp.logical_not(second) & (row > 0))
        def _():
            state_copy(j, 1).wait_recv()

        state = entering(j)
        back_out[0, j] = state.astype(BF16)
        for block in range(1, RING):
            state = state * factor(block - 1, j) + sum_in[block - 1, j].astype(F32)
            back_out[block, j] = state.astype(BF16)
        for distance in (2, 1, 3, 0):
            back_copy((place + distance) % RING, place, j).start()

    def within(j):
        cols = columns(cum_cols, j)
        for q in range(RING):
            chunk = q * CHUNKS + j
            score = scores[chunk // GROUP_CHUNKS]
            for p in range(PAIRS):
                at = pair_lanes(chunk, p)
                weights = []
                for k in range(2):
                    lane_at = q * (HEADS // RING) + 2 * p + k
                    decay = jnp.broadcast_to(cols[:, lane_at : lane_at + 1], (SPAN, SPAN))
                    row_at = pl.ds(chunk * CHUNK_HEADS + 2 * p + k, 1)
                    weight = score * jnp.exp2(decay - shift_rows[row_at, :])
                    weights.append(jnp.where(causal, weight, 0.0).astype(BF16))
                both = mixed[:, at]
                nothing = jnp.zeros_like(both)
                apart = jnp.concatenate(
                    [jnp.where(low, both, nothing), jnp.where(low, nothing, both)], axis=0
                )
                inner = jnp.dot(
                    jnp.concatenate(weights, axis=1), apart, preferred_element_type=F32
                )
                head = chunk * CHUNK_HEADS + 2 * p
                skip = jnp.where(low[:1], skip_ref[0, head], skip_ref[0, head + 1])
                part = x_ref[:, at].astype(F32) + inner + skip * both.astype(F32)
                part_out[chunk, :, p * 128 : (p + 1) * 128] = part.astype(BF16)
        for q in range(RING):
            part_copy(q * CHUNKS + j).start()

    def spread_decay(j):
        cols = columns(cum_in, j)
        for q in range(RING):
            chunk = q * CHUNKS + j
            for p in range(PAIRS):
                lane_at = q * (HEADS // RING) + 2 * p
                spread = jnp.where(
                    low, cols[:, lane_at : lane_at + 1], cols[:, lane_at + 1 : lane_at + 2]
                )
                grown[:, pair_lanes(chunk, p)] = jnp.exp2(spread)

    def finish(j):
        for q in range(RING):
            back_copy(place, q, j).wait_recv()
            part_copy(q * CHUNKS + j).wait_recv()
        for q in range(RING):
            chunk = q * CHUNKS + j
            lanes = lanes_of(chunk)
            group = pl.ds(pl.multiple_of((chunk // GROUP_CHUNKS) * STATE, STATE), STATE)
            carried = jnp.dot(read_in[:, group], back_in[q, j], preferred_element_type=F32)
            out_ref[:, lanes] = (part_in[chunk].astype(F32) + grown[:, lanes] * carried).astype(
                BF16
            )

    relay_lag = jnp.where(second, jnp.minimum(ODD + row, CHUNKS), EVEN)
    back_lag = jnp.where(second, jnp.maximum(relay_lag + LAG - row, CHUNKS), EVEN + LAG)
    finish_lag = back_lag + LATER

    def only(j, step):
        @pl.when((j >= 0) & (j < CHUNKS))
        def _():
            step(j)

    def pipeline(i, carry):
        only(i, produce)

        @pl.when(i == 2)
        def _():
            for distance in range(1, RING):
                source = (place + distance) % RING
                end_copy(source, place).wait_send()
                end_copy(source, source).wait_recv()
            for copy in map_copies(0, 1):
                copy.wait()

            @pl.when(jnp.logical_not(second))
            def _():
                fade_out[...] = (end_in[0] + end_in[1]) + (end_in[2] + end_in[3])
                fade_copy().start()

            @pl.when(second)
            def _():
                fade_copy().wait_recv()

        only(i - relay_lag, relay)
        only(i - back_lag, hand_back)
        only(i, within)
        only(i - 2, spread_decay)
        only(i - finish_lag, finish)
        return carry

    lax.fori_loop(0, CHUNKS + finish_lag, pipeline, 0)

    def settle(j, carry):
        for distance in range(1, RING):
            to = (place + distance) % RING
            sum_copy(to, place, j).wait_send()

        for to in range(RING):
            back_copy(to, place, j).wait_send()

        @pl.when(ctx < blocks - 1)
        def _():
            halo_copy(j).wait_send()

        @pl.when(passes_on)
        def _():
            state_copy(j, 2).wait_send()
            state_copy(j, 1).wait_send()

        @pl.when(jnp.logical_not(second))
        def _():
            front_copy(j).wait_send()

        for q in range(RING):
            part_copy(q * CHUNKS + j).wait_send()
        return carry

    lax.fori_loop(0, CHUNKS, settle, 0)

    @pl.when(jnp.logical_not(second))
    def _():
        fade_copy().wait_send()


def shards(
    section_input, norm_gain, conv_weight, state_write, state_read, step_size, log_decay, skip_gain
):
    hbm = pl.BlockSpec(memory_space=pltpu.HBM)
    dma = pltpu.SemaphoreType.DMA
    chunks = WIDTH // LANES
    half = (RING, CHUNKS, STATE, LANES)
    halo = (CHUNKS, RING, 8, 128)
    handed = pl.pallas_call(
        mixing_kernel,
        out_shape=jax.ShapeDtypeStruct((SPAN, WIDTH), BF16),
        in_specs=[hbm] * 7 + [pl.BlockSpec(memory_space=pltpu.SMEM)],
        out_specs=pl.BlockSpec(memory_space=pltpu.VMEM),
        scratch_shapes=[
            pltpu.VMEM((SPAN, WIDTH), BF16),
            pltpu.VMEM((1, WIDTH), BF16),
            pltpu.VMEM((CONV, WIDTH), BF16),
            pltpu.VMEM((SPAN, GROUPS * STATE), BF16),
            pltpu.VMEM((SPAN, GROUPS * STATE), BF16),
            pltpu.VMEM((HEADS, SPAN), F32),
            pltpu.VMEM((HEADS, SPAN), F32),
            pltpu.VMEM((SPAN, 128), F32),
            pltpu.VMEM((RING * PAIRS, SPAN + 8, 128), F32),
            pltpu.VMEM((SPAN, WIDTH), BF16),
            pltpu.VMEM((SPAN, WIDTH), F32),
            pltpu.VMEM((GROUPS, SPAN, SPAN), F32),
            pltpu.VMEM((GROUPS, STATE, SPAN), BF16),
            pltpu.VMEM((HEADS, SPAN), F32),
            pltpu.VMEM((SPAN, HEADS), F32),
            pltpu.VMEM((HEADS, SPAN), F32),
            pltpu.VMEM((SPAN, HEADS), F32),
            pltpu.VMEM(halo, F32),
            pltpu.VMEM(halo, F32),
            pltpu.VMEM((RING, CHUNKS * PAIRS, 128), F32),
            pltpu.VMEM((RING, CHUNKS * PAIRS, 128), F32),
            pltpu.VMEM(half, BF16),
            pltpu.VMEM(half, BF16),
            pltpu.VMEM(half[1:], BF16),
            pltpu.VMEM(half[1:], BF16),
            pltpu.VMEM(half[1:], BF16),
            pltpu.VMEM(half[1:], BF16),
            pltpu.VMEM((CHUNKS * PAIRS, 128), F32),
            pltpu.VMEM((CHUNKS * PAIRS, 128), F32),
            pltpu.VMEM(half, BF16),
            pltpu.VMEM(half, BF16),
            pltpu.VMEM((chunks, SPAN, LANES), BF16),
            pltpu.VMEM((chunks, SPAN, LANES), BF16),
            pltpu.VMEM((SPAN, GROUPS * STATE), BF16),
            pltpu.VMEM((SPAN, HEADS), F32),
            dma((8,)),
            dma((2, CHUNKS)),
            dma((2, RING)),
            dma((2, RING, CHUNKS)),
            dma((3, CHUNKS)),
            dma((2, CHUNKS)),
            dma((2,)),
            dma((2, RING, CHUNKS)),
            dma((2, chunks)),
            dma((2, 2)),
        ],
        compiler_params=pltpu.CompilerParams(
            collective_id=0, has_side_effects=True, vmem_limit_bytes=48 << 20
        ),
    )(
        *(
            pltpu.with_memory_space_constraint(operand, pltpu.HBM)
            for operand in (
                section_input[0],
                norm_gain,
                conv_weight[0],
                state_write[0],
                state_read[0],
                step_size[0],
                log_decay[0],
            )
        ),
        skip_gain,
    )
    return handed[None]


def solution(mesh):
    in_specs = (
        P("section", "ctx", None),
        P("section", None),
        P("section", None, None),
        P("section", "ctx", None),
        P("section", "ctx", None),
        P("section", None, "ctx"),
        P("section", None, "ctx"),
        P("section", None),
    )
    out_specs = P("section", "ctx", None)
    return jax.shard_map(shards, mesh=mesh, in_specs=in_specs, out_specs=out_specs, check_vma=False)
```

```python
import jax
import jax.numpy as jnp
from jax import lax
from jax.experimental import pallas as pl
from jax.experimental.pallas import tpu as pltpu
from jax.sharding import PartitionSpec as P

HEADS = 128
HEAD_DIM = 64
STATE = 128
GROUPS = 8
CONV = 4
SPAN = 128
WIDTH = HEADS * HEAD_DIM
RING = 4
LANES = 256
PAIRS = LANES // 128
CHUNK_HEADS = LANES // HEAD_DIM
CHUNKS = WIDTH // RING // LANES
GROUP_CHUNKS = WIDTH // GROUPS // LANES
LATER = 3
EVEN = 3
ODD = 3
LAG = 5
LOG2E = 1.4426950408889634
F32 = jnp.float32
BF16 = jnp.bfloat16


def mixing_kernel(
    x_hbm, gain_hbm, taps_hbm, write_hbm, read_hbm, step_hbm, decay_hbm, skip_hbm,
    out_ref,
    x_ref, gain_ref, taps_ref, write_ref, read_ref, step_ref, decay_ref, skip_ref,
    scale_buf, padded, mixed, grown, scores, write_t, cum_rows, cum_cols, shift_rows, shift_cols,
    halo_out, halo_in, end_out, end_in, sum_out, sum_in, state_in, state_out,
    front_out, front_in, fade_out, fade_in,
    back_out, back_in, part_out, part_in, read_in, cum_in,
    fetch_sems, halo_sems, end_sems, sum_sems, state_sems, front_sems, fade_sems, back_sems, part_sems, map_sems,
):
    sections, blocks = lax.axis_size("section"), lax.axis_size("ctx")
    rows = blocks // RING
    section, ctx = lax.axis_index("section"), lax.axis_index("ctx")
    row, place = ctx // RING, ctx % RING
    second = row % 2 == 1
    passes_on = second & (row < rows - 1)

    def at_ctx(index):
        return {"section": section, "ctx": index}

    def at_place(index):
        return at_ctx(row * RING + index)

    before_ctx, after_ctx = (ctx + blocks - 1) % blocks, (ctx + 1) % blocks
    before_section, after_section = (section + sections - 1) % sections, (section + 1) % sections

    def next_layer(index):
        return {"section": after_section, "ctx": row * RING + index}

    barrier = pltpu.get_barrier_semaphore()
    for index in range(RING):
        holder = {"section": before_section, "ctx": row * RING + index}
        pl.semaphore_signal(barrier, 1, device_id=holder)
    for distance in range(1, RING):
        pl.semaphore_signal(barrier, 1, device_id=at_place((place + distance) % RING))

    @pl.when(ctx > 0)
    def _():
        pl.semaphore_signal(barrier, 1, device_id=at_ctx(before_ctx))

    @pl.when(row > 0)
    def _():
        pl.semaphore_signal(barrier, 1, device_id=at_ctx(ctx - RING))

    @pl.when(second & (row > 1))
    def _():
        pl.semaphore_signal(barrier, 1, device_id=at_ctx(ctx - 2 * RING))

    late = SPAN - 16
    fetches = [
        pltpu.make_async_copy(source, target, fetch_sems.at[i])
        for i, (source, target) in enumerate(
            [
                (x_hbm.at[pl.ds(late, 16)], x_ref.at[pl.ds(late, 16)]),
                (gain_hbm, gain_ref),
                (decay_hbm, decay_ref),
                (step_hbm, step_ref),
                (x_hbm.at[pl.ds(0, late)], x_ref.at[pl.ds(0, late)]),
                (taps_hbm, taps_ref),
                (write_hbm, write_ref),
                (read_hbm, read_ref),
                (skip_hbm, skip_ref),
            ]
        )
    ]
    for fetch in fetches:
        fetch.start()

    def halo_copy(j):
        return pltpu.make_async_remote_copy(
            src_ref=halo_out.at[j], dst_ref=halo_in.at[j],
            send_sem=halo_sems.at[0, j], recv_sem=halo_sems.at[1, j],
            device_id=at_ctx(after_ctx),
        )

    def end_copy(to, slot):
        return pltpu.make_async_remote_copy(
            src_ref=end_out.at[to], dst_ref=end_in.at[slot],
            send_sem=end_sems.at[0, to], recv_sem=end_sems.at[1, slot], device_id=at_place(to),
        )

    def sum_copy(to, slot, j):
        return pltpu.make_async_remote_copy(
            src_ref=sum_out.at[to, j], dst_ref=sum_in.at[slot, j],
            send_sem=sum_sems.at[0, to, j], recv_sem=sum_sems.at[1, slot, j],
            device_id=at_place(to),
        )

    def state_copy(j, hops):
        return pltpu.make_async_remote_copy(
            src_ref=state_out.at[j], dst_ref=state_in.at[j],
            send_sem=state_sems.at[hops, j], recv_sem=state_sems.at[0, j],
            device_id=at_ctx((ctx + hops * RING) % blocks),
        )

    def front_copy(j):
        return pltpu.make_async_remote_copy(
            src_ref=front_out.at[j], dst_ref=front_in.at[j],
            send_sem=front_sems.at[0, j], recv_sem=front_sems.at[1, j],
            device_id=at_ctx((ctx + RING) % blocks),
        )

    def fade_copy():
        return pltpu.make_async_remote_copy(
            src_ref=fade_out, dst_ref=fade_in, send_sem=fade_sems.at[0], recv_sem=fade_sems.at[1],
            device_id=at_ctx((ctx + RING) % blocks),
        )

    def back_copy(to, slot, j):
        return pltpu.make_async_remote_copy(
            src_ref=back_out.at[to, j], dst_ref=back_in.at[slot, j],
            send_sem=back_sems.at[0, to, j], recv_sem=back_sems.at[1, slot, j],
            device_id=next_layer(to),
        )

    def lanes_of(chunk):
        return pl.ds(pl.multiple_of(chunk * LANES, LANES), LANES)

    def part_copy(chunk):
        return pltpu.make_async_remote_copy(
            src_ref=part_out.at[chunk], dst_ref=part_in.at[chunk],
            send_sem=part_sems.at[0, chunk], recv_sem=part_sems.at[1, chunk],
            device_id=next_layer(place),
        )

    def map_copies(*which):
        return [
            pltpu.make_async_remote_copy(
                src_ref=source, dst_ref=target,
                send_sem=map_sems.at[0, i], recv_sem=map_sems.at[1, i],
                device_id=next_layer(place),
            )
            for i, (source, target) in enumerate([(cum_cols, cum_in), (read_ref, read_in)])
            if i in which
        ]

    def square_sum(first, count):
        def add(i, acc):
            part = x_ref[pl.ds(first, count), pl.ds(pl.multiple_of(i * 1024, 1024), 1024)]
            for k in range(8):
                piece = part[:, k * 128 : (k + 1) * 128].astype(F32)
                acc = acc + piece * piece
            return acc

        acc = lax.fori_loop(0, WIDTH // 1024, add, jnp.zeros((count, 128), F32))
        mean = jnp.sum(acc, axis=-1, keepdims=True) * (1.0 / WIDTH)
        return jnp.broadcast_to(lax.rsqrt(mean + 1e-05), (count, 128))

    fetches[0].wait()
    fetches[1].wait()
    tail_scale = square_sum(late, 16)
    for chunk in range(RING * CHUNKS):
        for p in range(PAIRS):
            span = slice(chunk * LANES + p * 128, chunk * LANES + p * 128 + 128)
            normed = (x_ref[late:SPAN, span].astype(F32) * tail_scale) * gain_ref[:, span].astype(F32)
            normed = normed.astype(BF16).astype(F32)
            halo_out[chunk % CHUNKS, chunk // CHUNKS, 4 * p : 4 * p + 3, :] = normed[13:16, :]

    pl.semaphore_wait(
        barrier,
        2 * RING - 1
        + jnp.where(ctx < blocks - 1, 1, 0)
        + jnp.where(second, jnp.where(row < rows - 1, 2, 0), 1),
    )

    @pl.when(ctx < blocks - 1)
    def _():
        for j in range(CHUNKS):
            halo_copy(j).start()

    @pl.when(ctx == 0)
    def _():
        halo_in[...] = jnp.zeros_like(halo_in)

    token = lax.broadcasted_iota(jnp.int32, (SPAN, SPAN), 0)
    lane = lax.broadcasted_iota(jnp.int32, (SPAN, SPAN), 1)
    low = lane < HEAD_DIM
    causal = token >= lane
    upper = jnp.where(token <= lane, 1.0, 0.0).astype(F32)
    fetches[2].wait()
    cumul = lax.dot_general(
        decay_ref[...], upper, (((1,), (0,)), ((), ())),
        precision=lax.Precision.HIGHEST, preferred_element_type=F32,
    ) * LOG2E
    cum_rows[...] = cumul
    even, odd = (
        jnp.broadcast_to(cum_rows[pl.ds(first, HEADS // 2, stride=2), :][:, SPAN - 1 :], (HEADS // 2, 128))
        for first in range(2)
    )
    end_out[...] = jnp.where(low[: HEADS // 2], even, odd).reshape(RING, CHUNKS * PAIRS, 128)
    for distance in range(1, RING):
        to = (place + distance) % RING
        end_copy(to, place).start()
    end_in[place] = end_out[place]
    cum_cols[...] = cumul.T
    map_copies(0)[0].start()
    fetches[3].wait()
    shift = cumul - jnp.log2(step_ref[...])
    shift_rows[...] = shift
    shift_cols[...] = shift.T

    fetches[4].wait()
    scale = square_sum(0, SPAN)
    for fetch in fetches[5:]:
        fetch.wait()
    map_copies(1)[0].start()

    for g in range(GROUPS):
        span = slice(g * STATE, (g + 1) * STATE)
        writes = write_ref[:, span]
        scores[g] = lax.dot_general(
            read_ref[:, span], writes, (((1,), (1,)), ((), ())), preferred_element_type=F32
        )
        write_t[g] = writes.astype(F32).T.astype(BF16)

    def columns(ref, j):
        return pltpu.roll(ref[...], (HEADS - j * CHUNK_HEADS) % HEADS, 1)

    def pair_lanes(chunk, p):
        return pl.ds(pl.multiple_of(chunk * LANES + p * 128, 128), 128)

    scale_buf[...] = scale

    def produce(j):
        for q in range(RING):
            for p in range(PAIRS):
                at = pair_lanes(q * CHUNKS + j, p)
                normed = (x_ref[:, at].astype(F32) * scale_buf[...]) * gain_ref[:, at].astype(F32)
                padded[q * PAIRS + p, 8:, :] = normed.astype(BF16).astype(F32)

        @pl.when(ctx > 0)
        def _():
            halo_copy(j).wait_recv()

        cols = columns(shift_cols, j)
        for q in range(RING):
            chunk = q * CHUNKS + j
            parts = []
            for p in range(PAIRS):
                at = pair_lanes(chunk, p)
                buffer = padded.at[q * PAIRS + p]
                buffer[8 - (CONV - 1) : 8, :] = halo_in[j, q, 4 * p : 4 * p + 3, :]
                taps = taps_ref[:, at].astype(F32)
                acc = taps[0:1, :] * buffer[8 - (CONV - 1) : 8 - (CONV - 1) + SPAN, :]
                for k in range(1, CONV):
                    first = 8 - (CONV - 1) + k
                    acc = acc + taps[k : k + 1, :] * buffer[first : first + SPAN, :]
                acc = acc * (0.5 + 0.5 * jnp.tanh(0.5 * acc))
                value = acc.astype(BF16)
                mixed[:, at] = value
                head = q * (HEADS // RING) + 2 * p
                spread = jnp.where(low, cols[:, head : head + 1], cols[:, head + 1 : head + 2])
                end = end_out[q, pl.ds(j * PAIRS + p, 1), :]
                parts.append((value.astype(F32) * jnp.exp2(end - spread)).astype(BF16))
            sum_out[q, j] = jnp.dot(
                write_t[chunk // GROUP_CHUNKS],
                jnp.concatenate(parts, axis=1),
                preferred_element_type=F32,
            ).astype(BF16)
        for distance in (2, 1, 3):
            sum_copy((place + distance) % RING, place, j).start()
        sum_in[place, j] = sum_out[place, j]

    @pl.when(row < 2)
    def _():
        state_in[...] = jnp.zeros_like(state_in)

    @pl.when(jnp.logical_not(second))
    def _():
        front_in[...] = jnp.zeros_like(front_in)
        fade_in[...] = jnp.zeros_like(fade_in)

    def spread_row(ref, j):
        return jnp.concatenate(
            [jnp.exp2(ref[pl.ds(j * PAIRS + p, 1), :]) for p in range(PAIRS)], axis=1
        )

    def factor(source, j):
        return spread_row(end_in.at[source], j)

    def relay(j):
        for distance in range(1, RING):
            source = (place + distance) % RING
            sum_copy(source, source, j).wait_recv()
        whole = factor(0, j)
        summed = sum_in[0, j].astype(F32)
        for block in range(1, RING):
            one = factor(block, j)
            whole = whole * one
            summed = summed * one + sum_in[block, j].astype(F32)

        @pl.when(jnp.logical_not(second))
        def _():
            front_out[j] = summed.astype(BF16)
            front_copy(j).start()

        @pl.when(second)
        def _():
            front_copy(j).wait_recv()

            @pl.when(row > 1)
            def _():
                state_copy(j, 1).wait_recv()

        @pl.when(passes_on)
        def _():
            state_out[j] = (entering(j) * whole + summed).astype(BF16)
            state_copy(j, 2).start()
            state_copy(j, 1).start()

    def entering(j):
        return state_in[j].astype(F32) * spread_row(fade_in, j) + front_in[j].astype(F32)

    def hand_back(j):
        @pl.when(jnp.logical_not(second) & (row > 0))
        def _():
            state_copy(j, 1).wait_recv()

        state = entering(j)
        back_out[0, j] = state.astype(BF16)
        for block in range(1, RING):
            state = state * factor(block - 1, j) + sum_in[block - 1, j].astype(F32)
            back_out[block, j] = state.astype(BF16)
        for distance in (2, 1, 3, 0):
            back_copy((place + distance) % RING, place, j).start()

    def within(j):
        cols = columns(cum_cols, j)
        for q in range(RING):
            chunk = q * CHUNKS + j
            score = scores[chunk // GROUP_CHUNKS]
            for p in range(PAIRS):
                at = pair_lanes(chunk, p)
                weights = []
                for k in range(2):
                    lane_at = q * (HEADS // RING) + 2 * p + k
                    decay = jnp.broadcast_to(cols[:, lane_at : lane_at + 1], (SPAN, SPAN))
                    row_at = pl.ds(chunk * CHUNK_HEADS + 2 * p + k, 1)
                    weight = score * jnp.exp2(decay - shift_rows[row_at, :])
                    weights.append(jnp.where(causal, weight, 0.0).astype(BF16))
                both = mixed[:, at]
                nothing = jnp.zeros_like(both)
                apart = jnp.concatenate(
                    [jnp.where(low, both, nothing), jnp.where(low, nothing, both)], axis=0
                )
                inner = jnp.dot(
                    jnp.concatenate(weights, axis=1), apart, preferred_element_type=F32
                )
                head = chunk * CHUNK_HEADS + 2 * p
                skip = jnp.where(low[:1], skip_ref[0, head], skip_ref[0, head + 1])
                part = x_ref[:, at].astype(F32) + inner + skip * both.astype(F32)
                part_out[chunk, :, p * 128 : (p + 1) * 128] = part.astype(BF16)
        for q in range(RING):
            part_copy(q * CHUNKS + j).start()

    def spread_decay(j):
        cols = columns(cum_in, j)
        for q in range(RING):
            chunk = q * CHUNKS + j
            for p in range(PAIRS):
                lane_at = q * (HEADS // RING) + 2 * p
                spread = jnp.where(
                    low, cols[:, lane_at : lane_at + 1], cols[:, lane_at + 1 : lane_at + 2]
                )
                grown[:, pair_lanes(chunk, p)] = jnp.exp2(spread)

    def finish(j):
        for q in range(RING):
            back_copy(place, q, j).wait_recv()
            part_copy(q * CHUNKS + j).wait_recv()
        for q in range(RING):
            chunk = q * CHUNKS + j
            lanes = lanes_of(chunk)
            group = pl.ds(pl.multiple_of((chunk // GROUP_CHUNKS) * STATE, STATE), STATE)
            carried = jnp.dot(read_in[:, group], back_in[q, j], preferred_element_type=F32)
            out_ref[:, lanes] = (part_in[chunk].astype(F32) + grown[:, lanes] * carried).astype(
                BF16
            )

    relay_lag = jnp.where(second, jnp.minimum(ODD + row, CHUNKS), EVEN)
    back_lag = jnp.where(second, jnp.maximum(relay_lag + LAG - row, CHUNKS), EVEN + LAG)
    finish_lag = back_lag + LATER

    def only(j, step):
        @pl.when((j >= 0) & (j < CHUNKS))
        def _():
            step(j)

    def pipeline(i, carry):
        only(i, produce)

        @pl.when(i == 2)
        def _():
            for distance in range(1, RING):
                source = (place + distance) % RING
                end_copy(source, place).wait_send()
                end_copy(source, source).wait_recv()
            for copy in map_copies(0, 1):
                copy.wait()

            @pl.when(jnp.logical_not(second))
            def _():
                fade_out[...] = (end_in[0] + end_in[1]) + (end_in[2] + end_in[3])
                fade_copy().start()

            @pl.when(second)
            def _():
                fade_copy().wait_recv()

        only(i - relay_lag, relay)
        only(i - back_lag, hand_back)
        only(i, within)
        only(i - 2, spread_decay)
        only(i - finish_lag, finish)
        return carry

    lax.fori_loop(0, CHUNKS + finish_lag, pipeline, 0)

    def settle(j, carry):
        for distance in range(1, RING):
            to = (place + distance) % RING
            sum_copy(to, place, j).wait_send()

        for to in range(RING):
            back_copy(to, place, j).wait_send()

        @pl.when(ctx < blocks - 1)
        def _():
            halo_copy(j).wait_send()

        @pl.when(passes_on)
        def _():
            state_copy(j, 2).wait_send()
            state_copy(j, 1).wait_send()

        @pl.when(jnp.logical_not(second))
        def _():
            front_copy(j).wait_send()

        for q in range(RING):
            part_copy(q * CHUNKS + j).wait_send()
        return carry

    lax.fori_loop(0, CHUNKS, settle, 0)

    @pl.when(jnp.logical_not(second))
    def _():
        fade_copy().wait_send()


def shards(
    section_input, norm_gain, conv_weight, state_write, state_read, step_size, log_decay, skip_gain
):
    hbm = pl.BlockSpec(memory_space=pltpu.HBM)
    dma = pltpu.SemaphoreType.DMA
    chunks = WIDTH // LANES
    half = (RING, CHUNKS, STATE, LANES)
    halo = (CHUNKS, RING, 8, 128)
    handed = pl.pallas_call(
        mixing_kernel,
        out_shape=jax.ShapeDtypeStruct((SPAN, WIDTH), BF16),
        in_specs=[hbm] * 8,
        out_specs=pl.BlockSpec(memory_space=pltpu.VMEM),
        scratch_shapes=[
            pltpu.VMEM((SPAN, WIDTH), BF16),
            pltpu.VMEM((1, WIDTH), BF16),
            pltpu.VMEM((CONV, WIDTH), BF16),
            pltpu.VMEM((SPAN, GROUPS * STATE), BF16),
            pltpu.VMEM((SPAN, GROUPS * STATE), BF16),
            pltpu.VMEM((HEADS, SPAN), F32),
            pltpu.VMEM((HEADS, SPAN), F32),
            pltpu.SMEM((1, HEADS), F32),
            pltpu.VMEM((SPAN, 128), F32),
            pltpu.VMEM((RING * PAIRS, SPAN + 8, 128), F32),
            pltpu.VMEM((SPAN, WIDTH), BF16),
            pltpu.VMEM((SPAN, WIDTH), F32),
            pltpu.VMEM((GROUPS, SPAN, SPAN), F32),
            pltpu.VMEM((GROUPS, STATE, SPAN), BF16),
            pltpu.VMEM((HEADS, SPAN), F32),
            pltpu.VMEM((SPAN, HEADS), F32),
            pltpu.VMEM((HEADS, SPAN), F32),
            pltpu.VMEM((SPAN, HEADS), F32),
            pltpu.VMEM(halo, F32),
            pltpu.VMEM(halo, F32),
            pltpu.VMEM((RING, CHUNKS * PAIRS, 128), F32),
            pltpu.VMEM((RING, CHUNKS * PAIRS, 128), F32),
            pltpu.VMEM(half, BF16),
            pltpu.VMEM(half, BF16),
            pltpu.VMEM(half[1:], BF16),
            pltpu.VMEM(half[1:], BF16),
            pltpu.VMEM(half[1:], BF16),
            pltpu.VMEM(half[1:], BF16),
            pltpu.VMEM((CHUNKS * PAIRS, 128), F32),
            pltpu.VMEM((CHUNKS * PAIRS, 128), F32),
            pltpu.VMEM(half, BF16),
            pltpu.VMEM(half, BF16),
            pltpu.VMEM((chunks, SPAN, LANES), BF16),
            pltpu.VMEM((chunks, SPAN, LANES), BF16),
            pltpu.VMEM((SPAN, GROUPS * STATE), BF16),
            pltpu.VMEM((SPAN, HEADS), F32),
            dma((9,)),
            dma((2, CHUNKS)),
            dma((2, RING)),
            dma((2, RING, CHUNKS)),
            dma((3, CHUNKS)),
            dma((2, CHUNKS)),
            dma((2,)),
            dma((2, RING, CHUNKS)),
            dma((2, chunks)),
            dma((2, 2)),
        ],
        compiler_params=pltpu.CompilerParams(
            collective_id=0, has_side_effects=True, vmem_limit_bytes=48 << 20
        ),
    )(
        *(
            pltpu.with_memory_space_constraint(operand, pltpu.HBM)
            for operand in (
                section_input[0],
                norm_gain,
                conv_weight[0],
                state_write[0],
                state_read[0],
                step_size[0],
                log_decay[0],
                skip_gain,
            )
        )
    )
    return handed[None]


def solution(mesh):
    in_specs = (
        P("section", "ctx", None),
        P("section", None),
        P("section", None, None),
        P("section", "ctx", None),
        P("section", "ctx", None),
        P("section", None, "ctx"),
        P("section", None, "ctx"),
        P("section", None),
    )
    out_specs = P("section", "ctx", None)
    return jax.shard_map(shards, mesh=mesh, in_specs=in_specs, out_specs=out_specs, check_vma=False)
```

```python
import jax
import jax.numpy as jnp
from jax import lax
from jax.experimental import pallas as pl
from jax.experimental.pallas import tpu as pltpu
from jax.sharding import PartitionSpec as P

HEADS = 128
HEAD_DIM = 64
STATE = 128
GROUPS = 8
CONV = 4
SPAN = 128
WIDTH = HEADS * HEAD_DIM
RING = 4
LANES = 256
PAIRS = LANES // 128
CHUNK_HEADS = LANES // HEAD_DIM
CHUNKS = WIDTH // RING // LANES
GROUP_CHUNKS = WIDTH // GROUPS // LANES
LATER = 3
EVEN = 3
ODD = 3
LAG = 5
END_ROWS = CHUNKS * PAIRS
LOG2E = 1.4426950408889634
F32 = jnp.float32
BF16 = jnp.bfloat16


def mixing_kernel(
    x_hbm, gain_hbm, taps_hbm, write_hbm, read_hbm, step_hbm, decay_hbm, skip_hbm,
    out_ref,
    x_ref, gain_ref, taps_ref, write_ref, read_ref, step_ref, decay_ref, skip_ref,
    scale_buf, padded, mixed, grown, scores, write_t, cum_rows, cum_cols, shift_rows, shift_cols,
    halo_out, halo_in, end_out, end_in, sum_out, sum_in, state_in, state_out,
    front_out, front_in, fade_out, fade_in,
    back_out, back_in, part_out, part_in, read_in, cum_in,
    fetch_sems, halo_sems, end_sems, sum_sems, state_sems, front_sems, fade_sems, back_sems, part_sems, map_sems,
):
    sections, blocks = lax.axis_size("section"), lax.axis_size("ctx")
    rows = blocks // RING
    section, ctx = lax.axis_index("section"), lax.axis_index("ctx")
    row, place = ctx // RING, ctx % RING
    second = row % 2 == 1
    passes_on = second & (row < rows - 1)

    def at_ctx(index):
        return {"section": section, "ctx": index}

    def at_place(index):
        return at_ctx(row * RING + index)

    before_ctx, after_ctx = (ctx + blocks - 1) % blocks, (ctx + 1) % blocks
    before_section, after_section = (section + sections - 1) % sections, (section + 1) % sections

    def next_layer(index):
        return {"section": after_section, "ctx": row * RING + index}

    barrier = pltpu.get_barrier_semaphore()
    for index in range(RING):
        holder = {"section": before_section, "ctx": row * RING + index}
        pl.semaphore_signal(barrier, 1, device_id=holder)
    for distance in range(1, RING):
        pl.semaphore_signal(barrier, 1, device_id=at_place((place + distance) % RING))

    @pl.when(ctx > 0)
    def _():
        pl.semaphore_signal(barrier, 1, device_id=at_ctx(before_ctx))

    @pl.when(row > 0)
    def _():
        pl.semaphore_signal(barrier, 1, device_id=at_ctx(ctx - RING))

    @pl.when(second & (row > 1))
    def _():
        pl.semaphore_signal(barrier, 1, device_id=at_ctx(ctx - 2 * RING))

    late = SPAN - 16
    fetches = [
        pltpu.make_async_copy(source, target, fetch_sems.at[i])
        for i, (source, target) in enumerate(
            [
                (x_hbm.at[pl.ds(late, 16)], x_ref.at[pl.ds(late, 16)]),
                (gain_hbm, gain_ref),
                (decay_hbm, decay_ref),
                (step_hbm, step_ref),
                (x_hbm.at[pl.ds(0, late)], x_ref.at[pl.ds(0, late)]),
                (taps_hbm, taps_ref),
                (write_hbm, write_ref),
                (read_hbm, read_ref),
                (skip_hbm, skip_ref),
            ]
        )
    ]
    for fetch in fetches:
        fetch.start()

    def halo_copy(j):
        return pltpu.make_async_remote_copy(
            src_ref=halo_out.at[j], dst_ref=halo_in.at[j],
            send_sem=halo_sems.at[0, j], recv_sem=halo_sems.at[1, j],
            device_id=at_ctx(after_ctx),
        )

    def end_copy(to, slot):
        return pltpu.make_async_remote_copy(
            src_ref=end_out.at[to, pl.ds(0, END_ROWS)], dst_ref=end_in.at[slot, pl.ds(0, END_ROWS)],
            send_sem=end_sems.at[0, to], recv_sem=end_sems.at[1, slot], device_id=at_place(to),
        )

    def sum_copy(to, slot, j):
        return pltpu.make_async_remote_copy(
            src_ref=sum_out.at[to, j], dst_ref=sum_in.at[slot, j],
            send_sem=sum_sems.at[0, to, j], recv_sem=sum_sems.at[1, slot, j],
            device_id=at_place(to),
        )

    def state_copy(j, hops):
        return pltpu.make_async_remote_copy(
            src_ref=state_out.at[j], dst_ref=state_in.at[j],
            send_sem=state_sems.at[hops, j], recv_sem=state_sems.at[0, j],
            device_id=at_ctx((ctx + hops * RING) % blocks),
        )

    def front_copy(j):
        return pltpu.make_async_remote_copy(
            src_ref=front_out.at[j], dst_ref=front_in.at[j],
            send_sem=front_sems.at[0, j], recv_sem=front_sems.at[1, j],
            device_id=at_ctx((ctx + RING) % blocks),
        )

    def fade_copy():
        return pltpu.make_async_remote_copy(
            src_ref=fade_out, dst_ref=fade_in.at[pl.ds(0, END_ROWS)], send_sem=fade_sems.at[0], recv_sem=fade_sems.at[1],
            device_id=at_ctx((ctx + RING) % blocks),
        )

    def back_copy(to, slot, j):
        return pltpu.make_async_remote_copy(
            src_ref=back_out.at[to, j], dst_ref=back_in.at[slot, j],
            send_sem=back_sems.at[0, to, j], recv_sem=back_sems.at[1, slot, j],
            device_id=next_layer(to),
        )

    def lanes_of(chunk):
        return pl.ds(pl.multiple_of(chunk * LANES, LANES), LANES)

    def part_copy(chunk):
        return pltpu.make_async_remote_copy(
            src_ref=part_out.at[chunk], dst_ref=part_in.at[chunk],
            send_sem=part_sems.at[0, chunk], recv_sem=part_sems.at[1, chunk],
            device_id=next_layer(place),
        )

    def map_copies(*which):
        return [
            pltpu.make_async_remote_copy(
                src_ref=source, dst_ref=target,
                send_sem=map_sems.at[0, i], recv_sem=map_sems.at[1, i],
                device_id=next_layer(place),
            )
            for i, (source, target) in enumerate([(cum_cols, cum_in), (read_ref, read_in)])
            if i in which
        ]

    def square_sum(first, count):
        def add(i, acc):
            part = x_ref[pl.ds(first, count), pl.ds(pl.multiple_of(i * 1024, 1024), 1024)]
            for k in range(8):
                piece = part[:, k * 128 : (k + 1) * 128].astype(F32)
                acc = acc + piece * piece
            return acc

        acc = lax.fori_loop(0, WIDTH // 1024, add, jnp.zeros((count, 128), F32))
        mean = jnp.sum(acc, axis=-1, keepdims=True) * (1.0 / WIDTH)
        return jnp.broadcast_to(lax.rsqrt(mean + 1e-05), (count, 128))

    fetches[0].wait()
    fetches[1].wait()
    tail_scale = square_sum(late, 16)
    for j in range(CHUNKS):
        for half in range(2):
            pieces = []
            for part in range(2 * PAIRS):
                q, p = 2 * half + part // PAIRS, part % PAIRS
                first = (q * CHUNKS + j) * LANES + p * 128
                span = slice(first, first + 128)
                normed = (x_ref[late:SPAN, span].astype(F32) * tail_scale) * gain_ref[
                    :, span
                ].astype(F32)
                pieces.append(normed[12:16, :])
            halo_out[j, half] = jnp.concatenate(pieces, axis=0).astype(BF16)

    pl.semaphore_wait(
        barrier,
        2 * RING - 1
        + jnp.where(ctx < blocks - 1, 1, 0)
        + jnp.where(second, jnp.where(row < rows - 1, 2, 0), 1),
    )

    @pl.when(ctx < blocks - 1)
    def _():
        for j in range(CHUNKS):
            halo_copy(j).start()

    @pl.when(ctx == 0)
    def _():
        halo_in[...] = jnp.zeros_like(halo_in)

    token = lax.broadcasted_iota(jnp.int32, (SPAN, SPAN), 0)
    lane = lax.broadcasted_iota(jnp.int32, (SPAN, SPAN), 1)
    low = lane < HEAD_DIM
    causal = token >= lane
    upper = jnp.where(token <= lane, 1.0, 0.0).astype(F32)
    fetches[2].wait()
    cumul = lax.dot_general(
        decay_ref[...], upper, (((1,), (0,)), ((), ())),
        precision=lax.Precision.HIGHEST, preferred_element_type=F32,
    ) * LOG2E
    cum_rows[...] = cumul
    even, odd = (
        jnp.broadcast_to(cum_rows[pl.ds(first, HEADS // 2, stride=2), :][:, SPAN - 1 :], (HEADS // 2, 128))
        for first in range(2)
    )
    ends = jnp.where(low[: HEADS // 2], even, odd)
    end_out[:, pl.ds(0, END_ROWS), :] = ends.reshape(RING, END_ROWS, 128)
    for distance in range(1, RING):
        to = (place + distance) % RING
        end_copy(to, place).start()
    end_in[place, pl.ds(0, END_ROWS), :] = end_out[place, pl.ds(0, END_ROWS), :]
    cum_cols[...] = cumul.T
    map_copies(0)[0].start()
    fetches[3].wait()
    shift = cumul - jnp.log2(step_ref[...])
    shift_rows[pl.ds(0, HEADS), :] = shift
    shift_cols[...] = shift.T

    fetches[4].wait()
    scale = square_sum(0, SPAN)
    for fetch in fetches[5:]:
        fetch.wait()
    map_copies(1)[0].start()

    for g in range(GROUPS):
        span = slice(g * STATE, (g + 1) * STATE)
        writes = write_ref[:, span]
        scores[g] = lax.dot_general(
            read_ref[:, span], writes, (((1,), (1,)), ((), ())), preferred_element_type=F32
        )
        write_t[g] = writes.astype(F32).T.astype(BF16)

    def columns(ref, j):
        return pltpu.roll(ref[...], (HEADS - j * CHUNK_HEADS) % HEADS, 1)

    def pair_lanes(chunk, p):
        return pl.ds(pl.multiple_of(chunk * LANES + p * 128, 128), 128)

    scale_buf[...] = scale

    def produce(j):
        for q in range(RING):
            for p in range(PAIRS):
                at = pair_lanes(q * CHUNKS + j, p)
                normed = (x_ref[:, at].astype(F32) * scale_buf[...]) * gain_ref[:, at].astype(F32)
                padded[q * PAIRS + p, 8:, :] = normed.astype(BF16).astype(F32)

        @pl.when(ctx > 0)
        def _():
            halo_copy(j).wait_recv()

        before = [halo_in[j, half].astype(F32) for half in range(2)]
        cols = columns(shift_cols, j)
        for q in range(RING):
            chunk = q * CHUNKS + j
            parts = []
            for p in range(PAIRS):
                at = pair_lanes(chunk, p)
                buffer = padded.at[q * PAIRS + p]
                first = 4 * (q % 2 * PAIRS + p)
                buffer[4:8, :] = before[q // 2][first : first + 4, :]
                taps = taps_ref[:, at].astype(F32)
                acc = taps[0:1, :] * buffer[8 - (CONV - 1) : 8 - (CONV - 1) + SPAN, :]
                for k in range(1, CONV):
                    first = 8 - (CONV - 1) + k
                    acc = acc + taps[k : k + 1, :] * buffer[first : first + SPAN, :]
                acc = acc * (0.5 + 0.5 * jnp.tanh(0.5 * acc))
                value = acc.astype(BF16)
                mixed[:, at] = value
                head = q * (HEADS // RING) + 2 * p
                spread = jnp.where(low, cols[:, head : head + 1], cols[:, head + 1 : head + 2])
                end = end_out[q, pl.ds(j * PAIRS + p, 1), :]
                parts.append((value.astype(F32) * jnp.exp2(end - spread)).astype(BF16))
            sum_out[q, j] = jnp.dot(
                write_t[chunk // GROUP_CHUNKS],
                jnp.concatenate(parts, axis=1),
                preferred_element_type=F32,
            ).astype(BF16)
        for distance in (2, 1, 3):
            sum_copy((place + distance) % RING, place, j).start()
        sum_in[place, j] = sum_out[place, j]

    @pl.when(row < 2)
    def _():
        state_in[...] = jnp.zeros_like(state_in)

    @pl.when(jnp.logical_not(second))
    def _():
        front_in[...] = jnp.zeros_like(front_in)
        fade_in[...] = jnp.zeros_like(fade_in)

    def spread_row(ref, j):
        return jnp.concatenate(
            [jnp.exp2(ref[pl.ds(j * PAIRS + p, 1), :]) for p in range(PAIRS)], axis=1
        )

    def factor(source, j):
        return spread_row(end_in.at[source], j)

    def relay(j):
        for distance in range(1, RING):
            source = (place + distance) % RING
            sum_copy(source, source, j).wait_recv()
        whole = factor(0, j)
        summed = sum_in[0, j].astype(F32)
        for block in range(1, RING):
            one = factor(block, j)
            whole = whole * one
            summed = summed * one + sum_in[block, j].astype(F32)

        @pl.when(jnp.logical_not(second))
        def _():
            front_out[j] = summed.astype(BF16)
            front_copy(j).start()

        @pl.when(second)
        def _():
            front_copy(j).wait_recv()

            @pl.when(row > 1)
            def _():
                state_copy(j, 1).wait_recv()

        @pl.when(passes_on)
        def _():
            state_out[j] = (entering(j) * whole + summed).astype(BF16)
            state_copy(j, 2).start()
            state_copy(j, 1).start()

    def entering(j):
        return state_in[j].astype(F32) * spread_row(fade_in, j) + front_in[j].astype(F32)

    def hand_back(j):
        @pl.when(jnp.logical_not(second) & (row > 0))
        def _():
            state_copy(j, 1).wait_recv()

        state = entering(j)
        back_out[0, j] = state.astype(BF16)
        for block in range(1, RING):
            state = state * factor(block - 1, j) + sum_in[block - 1, j].astype(F32)
            back_out[block, j] = state.astype(BF16)
        for distance in (2, 1, 3, 0):
            back_copy((place + distance) % RING, place, j).start()

    def within(j):
        cols = columns(cum_cols, j)
        for q in range(RING):
            chunk = q * CHUNKS + j
            score = scores[chunk // GROUP_CHUNKS]
            for p in range(PAIRS):
                at = pair_lanes(chunk, p)
                weights = []
                for k in range(2):
                    lane_at = q * (HEADS // RING) + 2 * p + k
                    decay = jnp.broadcast_to(cols[:, lane_at : lane_at + 1], (SPAN, SPAN))
                    row_at = pl.ds(chunk * CHUNK_HEADS + 2 * p + k, 1)
                    weight = score * jnp.exp2(decay - shift_rows[row_at, :])
                    weights.append(jnp.where(causal, weight, 0.0).astype(BF16))
                both = mixed[:, at]
                nothing = jnp.zeros_like(both)
                apart = jnp.concatenate(
                    [jnp.where(low, both, nothing), jnp.where(low, nothing, both)], axis=0
                )
                inner = jnp.dot(
                    jnp.concatenate(weights, axis=1), apart, preferred_element_type=F32
                )
                head = chunk * CHUNK_HEADS + 2 * p
                skip = jnp.where(low[:1], skip_ref[0, head], skip_ref[0, head + 1])
                part = x_ref[:, at].astype(F32) + inner + skip * both.astype(F32)
                part_out[chunk, :, p * 128 : (p + 1) * 128] = part.astype(BF16)
        for q in range(RING):
            part_copy(q * CHUNKS + j).start()

    def spread_decay(j):
        cols = columns(cum_in, j)
        for q in range(RING):
            chunk = q * CHUNKS + j
            for p in range(PAIRS):
                lane_at = q * (HEADS // RING) + 2 * p
                spread = jnp.where(
                    low, cols[:, lane_at : lane_at + 1], cols[:, lane_at + 1 : lane_at + 2]
                )
                grown[:, pair_lanes(chunk, p)] = jnp.exp2(spread)

    def finish(j):
        for distance in (0, 1, 3, 2):
            q = (place + distance) % RING
            chunk = q * CHUNKS + j
            lanes = lanes_of(chunk)
            group = pl.ds(pl.multiple_of((chunk // GROUP_CHUNKS) * STATE, STATE), STATE)
            part_copy(chunk).wait_recv()
            back_copy(place, q, j).wait_recv()
            carried = jnp.dot(read_in[:, group], back_in[q, j], preferred_element_type=F32)
            out_ref[:, lanes] = (part_in[chunk].astype(F32) + grown[:, lanes] * carried).astype(
                BF16
            )

    def settle(j):
        for distance in range(1, RING):
            to = (place + distance) % RING
            sum_copy(to, place, j).wait_send()

        for to in range(RING):
            back_copy(to, place, j).wait_send()

        @pl.when(ctx < blocks - 1)
        def _():
            halo_copy(j).wait_send()

        @pl.when(passes_on)
        def _():
            state_copy(j, 2).wait_send()
            state_copy(j, 1).wait_send()

        @pl.when(jnp.logical_not(second))
        def _():
            front_copy(j).wait_send()

        for q in range(RING):
            part_copy(q * CHUNKS + j).wait_send()

    relay_lag = jnp.where(second, jnp.minimum(ODD + row, CHUNKS), EVEN)
    back_lag = jnp.where(second, jnp.maximum(relay_lag + LAG - row, CHUNKS), EVEN + LAG)
    finish_lag = back_lag + LATER

    def only(j, step):
        @pl.when((j >= 0) & (j < CHUNKS))
        def _():
            step(j)

    def pipeline(i, carry):
        only(i, produce)

        @pl.when(i == 2)
        def _():
            for distance in range(1, RING):
                source = (place + distance) % RING
                end_copy(source, place).wait_send()
                end_copy(source, source).wait_recv()
            for copy in map_copies(0, 1):
                copy.wait()

            @pl.when(jnp.logical_not(second))
            def _():
                ends = [end_in[block, pl.ds(0, END_ROWS), :] for block in range(RING)]
                fade_out[...] = (ends[0] + ends[1]) + (ends[2] + ends[3])
                fade_copy().start()

            @pl.when(second)
            def _():
                fade_copy().wait_recv()

        only(i - relay_lag, relay)
        only(i - back_lag, hand_back)
        only(i, within)
        only(i - 2, spread_decay)
        only(i - finish_lag, settle)
        only(i - finish_lag, finish)
        return carry

    lax.fori_loop(0, CHUNKS + finish_lag, pipeline, 0)

    @pl.when(jnp.logical_not(second))
    def _():
        fade_copy().wait_send()


def shards(
    section_input, norm_gain, conv_weight, state_write, state_read, step_size, log_decay, skip_gain
):
    hbm = pl.BlockSpec(memory_space=pltpu.HBM)
    dma = pltpu.SemaphoreType.DMA
    chunks = WIDTH // LANES
    half = (RING, CHUNKS, STATE, LANES)
    halo = (CHUNKS, 2, 16, 128)
    handed = pl.pallas_call(
        mixing_kernel,
        out_shape=jax.ShapeDtypeStruct((SPAN, WIDTH), BF16),
        in_specs=[hbm] * 8,
        out_specs=pl.BlockSpec(memory_space=pltpu.VMEM),
        scratch_shapes=[
            pltpu.VMEM((SPAN, WIDTH), BF16),
            pltpu.VMEM((1, WIDTH), BF16),
            pltpu.VMEM((CONV, WIDTH), BF16),
            pltpu.VMEM((SPAN, GROUPS * STATE), BF16),
            pltpu.VMEM((SPAN, GROUPS * STATE), BF16),
            pltpu.VMEM((HEADS, SPAN), F32),
            pltpu.VMEM((HEADS, SPAN), F32),
            pltpu.SMEM((1, HEADS), F32),
            pltpu.VMEM((SPAN, 128), F32),
            pltpu.VMEM((RING * PAIRS, SPAN + 8, 128), F32),
            pltpu.VMEM((SPAN, WIDTH), BF16),
            pltpu.VMEM((SPAN, WIDTH), F32),
            pltpu.VMEM((GROUPS, SPAN, SPAN), F32),
            pltpu.VMEM((GROUPS, STATE, SPAN), BF16),
            pltpu.VMEM((HEADS, SPAN), F32),
            pltpu.VMEM((SPAN, HEADS), F32),
            pltpu.VMEM((HEADS + 8, SPAN), F32),
            pltpu.VMEM((SPAN, HEADS), F32),
            pltpu.VMEM(halo, BF16),
            pltpu.VMEM(halo, BF16),
            pltpu.VMEM((RING, END_ROWS + 8, 128), F32),
            pltpu.VMEM((RING, END_ROWS + 8, 128), F32),
            pltpu.VMEM(half, BF16),
            pltpu.VMEM(half, BF16),
            pltpu.VMEM(half[1:], BF16),
            pltpu.VMEM(half[1:], BF16),
            pltpu.VMEM(half[1:], BF16),
            pltpu.VMEM(half[1:], BF16),
            pltpu.VMEM((END_ROWS, 128), F32),
            pltpu.VMEM((END_ROWS + 8, 128), F32),
            pltpu.VMEM(half, BF16),
            pltpu.VMEM(half, BF16),
            pltpu.VMEM((chunks, SPAN, LANES), BF16),
            pltpu.VMEM((chunks, SPAN, LANES), BF16),
            pltpu.VMEM((SPAN, GROUPS * STATE), BF16),
            pltpu.VMEM((SPAN, HEADS), F32),
            dma((9,)),
            dma((2, CHUNKS)),
            dma((2, RING)),
            dma((2, RING, CHUNKS)),
            dma((3, CHUNKS)),
            dma((2, CHUNKS)),
            dma((2,)),
            dma((2, RING, CHUNKS)),
            dma((2, chunks)),
            dma((2, 2)),
        ],
        compiler_params=pltpu.CompilerParams(
            collective_id=0, has_side_effects=True, vmem_limit_bytes=48 << 20
        ),
    )(
        *(
            pltpu.with_memory_space_constraint(operand, pltpu.HBM)
            for operand in (
                section_input[0],
                norm_gain,
                conv_weight[0],
                state_write[0],
                state_read[0],
                step_size[0],
                log_decay[0],
                skip_gain,
            )
        )
    )
    return handed[None]


def solution(mesh):
    in_specs = (
        P("section", "ctx", None),
        P("section", None),
        P("section", None, None),
        P("section", "ctx", None),
        P("section", "ctx", None),
        P("section", None, "ctx"),
        P("section", None, "ctx"),
        P("section", None),
    )
    out_specs = P("section", "ctx", None)
    return jax.shard_map(shards, mesh=mesh, in_specs=in_specs, out_specs=out_specs, check_vma=False)
```

```python
import jax
import jax.numpy as jnp
from jax import lax
from jax.experimental import pallas as pl
from jax.experimental.pallas import tpu as pltpu
from jax.sharding import PartitionSpec as P

HEADS = 128
HEAD_DIM = 64
STATE = 128
GROUPS = 8
CONV = 4
SPAN = 128
WIDTH = HEADS * HEAD_DIM
RING = 4
LANES = 256
PAIRS = LANES // 128
CHUNK_HEADS = LANES // HEAD_DIM
CHUNKS = WIDTH // RING // LANES
GROUP_CHUNKS = WIDTH // GROUPS // LANES
LATER = 3
EVEN = 3
ODD = 3
LAG = 5
END_ROWS = CHUNKS * PAIRS
LOG2E = 1.4426950408889634
F32 = jnp.float32
BF16 = jnp.bfloat16


def mixing_kernel(
    x_hbm, gain_hbm, taps_hbm, write_hbm, read_hbm, step_hbm, decay_hbm, skip_hbm,
    out_ref,
    x_ref, gain_ref, taps_ref, write_ref, read_ref, step_ref, decay_ref, skip_ref,
    scale_buf, padded, mixed, grown, scores, write_t, cum_rows, cum_cols, shift_rows, shift_cols,
    halo_out, halo_in, end_out, end_in, sum_out, sum_in, state_in, state_out,
    front_out, front_in, fade_out, fade_in, head_out, head_in,
    back_out, back_in, part_out, part_in, read_in, cum_in,
    fetch_sems, halo_sems, end_sems, head_sems, sum_sems, state_sems, front_sems, fade_sems, back_sems, part_sems, map_sems,
):
    sections, blocks = lax.axis_size("section"), lax.axis_size("ctx")
    rows = blocks // RING
    section, ctx = lax.axis_index("section"), lax.axis_index("ctx")
    row, place = ctx // RING, ctx % RING
    second = row % 2 == 1
    passes_on = second & (row < rows - 1)

    def at_ctx(index):
        return {"section": section, "ctx": index}

    def at_place(index):
        return at_ctx(row * RING + index)

    before_ctx, after_ctx = (ctx + blocks - 1) % blocks, (ctx + 1) % blocks
    before_section, after_section = (section + sections - 1) % sections, (section + 1) % sections

    def next_layer(index):
        return {"section": after_section, "ctx": row * RING + index}

    barrier = pltpu.get_barrier_semaphore()
    for index in range(RING):
        holder = {"section": before_section, "ctx": row * RING + index}
        pl.semaphore_signal(barrier, 1, device_id=holder)
    for distance in range(1, RING):
        pl.semaphore_signal(barrier, 1, device_id=at_place((place + distance) % RING))

    @pl.when(ctx > 0)
    def _():
        pl.semaphore_signal(barrier, 1, device_id=at_ctx(before_ctx))

    @pl.when(row > 0)
    def _():
        pl.semaphore_signal(barrier, 1, device_id=at_ctx(ctx - RING))

    @pl.when(second & (row > 1))
    def _():
        pl.semaphore_signal(barrier, 1, device_id=at_ctx(ctx - 2 * RING))

    late = SPAN - 16
    fetches = [
        pltpu.make_async_copy(source, target, fetch_sems.at[i])
        for i, (source, target) in enumerate(
            [
                (x_hbm.at[pl.ds(late, 16)], x_ref.at[pl.ds(late, 16)]),
                (gain_hbm, gain_ref),
                (decay_hbm, decay_ref),
                (step_hbm, step_ref),
                (x_hbm.at[pl.ds(0, late)], x_ref.at[pl.ds(0, late)]),
                (taps_hbm, taps_ref),
                (write_hbm, write_ref),
                (read_hbm, read_ref),
                (skip_hbm, skip_ref),
            ]
        )
    ]
    for fetch in fetches:
        fetch.start()

    def halo_copy(j):
        return pltpu.make_async_remote_copy(
            src_ref=halo_out.at[j], dst_ref=halo_in.at[j],
            send_sem=halo_sems.at[0, j], recv_sem=halo_sems.at[1, j],
            device_id=at_ctx(after_ctx),
        )

    def end_copy(to, slot):
        return pltpu.make_async_remote_copy(
            src_ref=end_out.at[to, pl.ds(0, END_ROWS)], dst_ref=end_in.at[slot, pl.ds(0, END_ROWS)],
            send_sem=end_sems.at[0, to], recv_sem=end_sems.at[1, slot], device_id=at_place(to),
        )

    def sum_copy(to, slot, j):
        return pltpu.make_async_remote_copy(
            src_ref=sum_out.at[to, j], dst_ref=sum_in.at[slot, j],
            send_sem=sum_sems.at[0, to, j], recv_sem=sum_sems.at[1, slot, j],
            device_id=at_place(to),
        )

    def head_copy(to, slot):
        return pltpu.make_async_remote_copy(
            src_ref=head_out.at[to], dst_ref=head_in.at[slot],
            send_sem=head_sems.at[0, to], recv_sem=head_sems.at[1, slot], device_id=at_place(to),
        )

    def state_copy(j, hops):
        return pltpu.make_async_remote_copy(
            src_ref=state_out.at[j], dst_ref=state_in.at[j],
            send_sem=state_sems.at[hops, j], recv_sem=state_sems.at[0, j],
            device_id=at_ctx((ctx + hops * RING) % blocks),
        )

    def front_copy(j):
        return pltpu.make_async_remote_copy(
            src_ref=front_out.at[j], dst_ref=front_in.at[j],
            send_sem=front_sems.at[0, j], recv_sem=front_sems.at[1, j],
            device_id=at_ctx((ctx + RING) % blocks),
        )

    def fade_copy():
        return pltpu.make_async_remote_copy(
            src_ref=fade_out, dst_ref=fade_in.at[pl.ds(0, END_ROWS)], send_sem=fade_sems.at[0], recv_sem=fade_sems.at[1],
            device_id=at_ctx((ctx + RING) % blocks),
        )

    def back_copy(to, slot, j):
        return pltpu.make_async_remote_copy(
            src_ref=back_out.at[to, j], dst_ref=back_in.at[slot, j],
            send_sem=back_sems.at[0, to, j], recv_sem=back_sems.at[1, slot, j],
            device_id=next_layer(to),
        )

    def lanes_of(chunk):
        return pl.ds(pl.multiple_of(chunk * LANES, LANES), LANES)

    def part_copy(chunk):
        return pltpu.make_async_remote_copy(
            src_ref=part_out.at[chunk], dst_ref=part_in.at[chunk],
            send_sem=part_sems.at[0, chunk], recv_sem=part_sems.at[1, chunk],
            device_id=next_layer(place),
        )

    def map_copies(*which):
        return [
            pltpu.make_async_remote_copy(
                src_ref=source, dst_ref=target,
                send_sem=map_sems.at[0, i], recv_sem=map_sems.at[1, i],
                device_id=next_layer(place),
            )
            for i, (source, target) in enumerate([(cum_cols, cum_in), (read_ref, read_in)])
            if i in which
        ]

    def square_sum(first, count):
        def add(i, acc):
            part = x_ref[pl.ds(first, count), pl.ds(pl.multiple_of(i * 1024, 1024), 1024)]
            for k in range(8):
                piece = part[:, k * 128 : (k + 1) * 128].astype(F32)
                acc = acc + piece * piece
            return acc

        acc = lax.fori_loop(0, WIDTH // 1024, add, jnp.zeros((count, 128), F32))
        mean = jnp.sum(acc, axis=-1, keepdims=True) * (1.0 / WIDTH)
        return jnp.broadcast_to(lax.rsqrt(mean + 1e-05), (count, 128))

    fetches[0].wait()
    fetches[1].wait()
    tail_scale = square_sum(late, 16)
    for j in range(CHUNKS):
        for half in range(2):
            pieces = []
            for part in range(2 * PAIRS):
                q, p = 2 * half + part // PAIRS, part % PAIRS
                first = (q * CHUNKS + j) * LANES + p * 128
                span = slice(first, first + 128)
                normed = (x_ref[late:SPAN, span].astype(F32) * tail_scale) * gain_ref[
                    :, span
                ].astype(F32)
                pieces.append(normed[12:16, :])
            halo_out[j, half] = jnp.concatenate(pieces, axis=0).astype(BF16)

    token = lax.broadcasted_iota(jnp.int32, (SPAN, SPAN), 0)
    lane = lax.broadcasted_iota(jnp.int32, (SPAN, SPAN), 1)
    low = lane < HEAD_DIM
    causal = token >= lane
    upper = jnp.where(token <= lane, 1.0, 0.0).astype(F32)
    fetches[2].wait()
    cumul = lax.dot_general(
        decay_ref[...], upper, (((1,), (0,)), ((), ())),
        precision=lax.Precision.HIGHEST, preferred_element_type=F32,
    ) * LOG2E
    cum_rows[...] = cumul
    even, odd = (
        jnp.broadcast_to(cum_rows[pl.ds(first, HEADS // 2, stride=2), :][:, SPAN - 1 :], (HEADS // 2, 128))
        for first in range(2)
    )
    ends = jnp.where(low[: HEADS // 2], even, odd)
    end_out[:, pl.ds(0, END_ROWS), :] = ends.reshape(RING, END_ROWS, 128)
    end_in[place, pl.ds(0, END_ROWS), :] = end_out[place, pl.ds(0, END_ROWS), :]
    cum_cols[...] = cumul.T
    fetches[3].wait()
    shift = cumul - jnp.log2(step_ref[...])
    shift_rows[pl.ds(0, HEADS), :] = shift
    shift_cols[...] = shift.T

    fetches[4].wait()
    scale = square_sum(0, SPAN)
    for fetch in fetches[5:]:
        fetch.wait()

    for g in range(GROUPS):
        writes = write_ref[:, g * STATE : (g + 1) * STATE]
        write_t[g] = writes.astype(F32).T.astype(BF16)

    def columns(ref, j):
        return pltpu.roll(ref[...], (HEADS - j * CHUNK_HEADS) % HEADS, 1)

    def pair_lanes(chunk, p):
        return pl.ds(pl.multiple_of(chunk * LANES + p * 128, 128), 128)

    scale_buf[...] = scale

    def norm_chunk(j):
        for q in range(RING):
            for p in range(PAIRS):
                at = pair_lanes(q * CHUNKS + j, p)
                normed = (x_ref[:, at].astype(F32) * scale_buf[...]) * gain_ref[:, at].astype(F32)
                padded[q * PAIRS + p, 8:, :] = normed.astype(BF16).astype(F32)

    def take_halo(j):
        @pl.when(ctx > 0)
        def _():
            halo_copy(j).wait_recv()

        before = [halo_in[j, half].astype(F32) for half in range(2)]
        for q in range(RING):
            for p in range(PAIRS):
                first = 4 * (q % 2 * PAIRS + p)
                padded[q * PAIRS + p, 4:8, :] = before[q // 2][first : first + 4, :]

    def mix(j, q, p, count, cols):
        at = pair_lanes(q * CHUNKS + j, p)
        buffer = padded.at[q * PAIRS + p]
        taps = taps_ref[:, at].astype(F32)
        acc = taps[0:1, :] * buffer[8 - (CONV - 1) : 8 - (CONV - 1) + count, :]
        for k in range(1, CONV):
            first = 8 - (CONV - 1) + k
            acc = acc + taps[k : k + 1, :] * buffer[first : first + count, :]
        acc = acc * (0.5 + 0.5 * jnp.tanh(0.5 * acc))
        value = acc.astype(BF16)
        mixed[pl.ds(0, count), at] = value
        head = q * (HEADS // RING) + 2 * p
        spread = jnp.where(
            low[:count], cols[:count, head : head + 1], cols[:count, head + 1 : head + 2]
        )
        end = end_out[q, pl.ds(j * PAIRS + p, 1), :]
        return value.astype(F32) * jnp.exp2(end - spread)

    def send_sums(j):
        for distance in (2, 1, 3):
            sum_copy((place + distance) % RING, place, j).start()
        sum_in[place, j] = sum_out[place, j]

    def summarize(j, kept):
        cols = columns(shift_cols, j)
        for q in range(RING):
            parts = [kept(mix(j, q, p, SPAN, cols)).astype(BF16) for p in range(PAIRS)]
            sum_out[q, j] = jnp.dot(
                write_t[(q * CHUNKS + j) // GROUP_CHUNKS],
                jnp.concatenate(parts, axis=1),
                preferred_element_type=F32,
            ).astype(BF16)
        send_sums(j)

    def produce(j):
        norm_chunk(j)
        take_halo(j)
        summarize(j, lambda scaled: scaled)

    def produce_first():
        for q in range(RING * PAIRS):
            padded[q, 0:8, :] = jnp.zeros((8, 128), F32)
        norm_chunk(0)
        summarize(0, lambda scaled: jnp.where(token >= CONV - 1, scaled, 0.0))

    def complete_first():
        take_halo(0)
        cols = columns(shift_cols, 0)
        for q in range(RING):
            parts = [
                jnp.where(token[:16] < CONV - 1, mix(0, q, p, 16, cols), 0.0).astype(BF16)
                for p in range(PAIRS)
            ]
            group = q * CHUNKS // GROUP_CHUNKS * STATE
            parts.append(write_ref[0:16, group : group + STATE])
            head_out[q] = jnp.concatenate(parts, axis=1)
        for distance in range(1, RING):
            head_copy((place + distance) % RING, place).start()
        head_in[place] = head_out[place]

    def add_first():
        for distance in range(1, RING):
            source = (place + distance) % RING
            head_copy(source, source).wait_recv()
            sum_copy(source, source, 0).wait_recv()
        for source in range(RING):
            maps = head_in[source, :, LANES:].astype(F32).T.astype(BF16)
            added = jnp.dot(maps, head_in[source, :, :LANES], preferred_element_type=F32)
            sum_in[source, 0] = (sum_in[source, 0].astype(F32) + added).astype(BF16)

    pl.semaphore_wait(
        barrier,
        2 * RING - 1
        + jnp.where(ctx < blocks - 1, 1, 0)
        + jnp.where(second, jnp.where(row < rows - 1, 2, 0), 1),
    )

    @pl.when(ctx < blocks - 1)
    def _():
        for j in range(CHUNKS):
            halo_copy(j).start()

    @pl.when(ctx == 0)
    def _():
        halo_in[...] = jnp.zeros_like(halo_in)

    for distance in range(1, RING):
        to = (place + distance) % RING
        end_copy(to, place).start()
    for copy in map_copies(0, 1):
        copy.start()

    produce_first()
    for g in range(GROUPS):
        span = slice(g * STATE, (g + 1) * STATE)
        scores[g] = lax.dot_general(
            read_ref[:, span], write_ref[:, span], (((1,), (1,)), ((), ())),
            preferred_element_type=F32,
        )
    complete_first()

    @pl.when(row < 2)
    def _():
        state_in[...] = jnp.zeros_like(state_in)

    @pl.when(jnp.logical_not(second))
    def _():
        front_in[...] = jnp.zeros_like(front_in)
        fade_in[...] = jnp.zeros_like(fade_in)

    def spread_row(ref, j):
        return jnp.concatenate(
            [jnp.exp2(ref[pl.ds(j * PAIRS + p, 1), :]) for p in range(PAIRS)], axis=1
        )

    def factor(source, j):
        return spread_row(end_in.at[source], j)

    def relay(j):
        @pl.when(j == 0)
        def _():
            add_first()

        @pl.when(j > 0)
        def _():
            for distance in range(1, RING):
                source = (place + distance) % RING
                sum_copy(source, source, j).wait_recv()

        whole = factor(0, j)
        summed = sum_in[0, j].astype(F32)
        for block in range(1, RING):
            one = factor(block, j)
            whole = whole * one
            summed = summed * one + sum_in[block, j].astype(F32)

        @pl.when(jnp.logical_not(second))
        def _():
            front_out[j] = summed.astype(BF16)
            front_copy(j).start()

        @pl.when(second)
        def _():
            front_copy(j).wait_recv()

            @pl.when(row > 1)
            def _():
                state_copy(j, 1).wait_recv()

        @pl.when(passes_on)
        def _():
            state_out[j] = (entering(j) * whole + summed).astype(BF16)
            state_copy(j, 2).start()
            state_copy(j, 1).start()

    def entering(j):
        return state_in[j].astype(F32) * spread_row(fade_in, j) + front_in[j].astype(F32)

    def hand_back(j):
        @pl.when(jnp.logical_not(second) & (row > 0))
        def _():
            state_copy(j, 1).wait_recv()

        state = entering(j)
        back_out[0, j] = state.astype(BF16)
        for block in range(1, RING):
            state = state * factor(block - 1, j) + sum_in[block - 1, j].astype(F32)
            back_out[block, j] = state.astype(BF16)
        for distance in (2, 1, 3, 0):
            back_copy((place + distance) % RING, place, j).start()

    def within(j):
        cols = columns(cum_cols, j)
        for q in range(RING):
            chunk = q * CHUNKS + j
            score = scores[chunk // GROUP_CHUNKS]
            for p in range(PAIRS):
                at = pair_lanes(chunk, p)
                weights = []
                for k in range(2):
                    lane_at = q * (HEADS // RING) + 2 * p + k
                    decay = jnp.broadcast_to(cols[:, lane_at : lane_at + 1], (SPAN, SPAN))
                    row_at = pl.ds(chunk * CHUNK_HEADS + 2 * p + k, 1)
                    weight = score * jnp.exp2(decay - shift_rows[row_at, :])
                    weights.append(jnp.where(causal, weight, 0.0).astype(BF16))
                both = mixed[:, at]
                nothing = jnp.zeros_like(both)
                apart = jnp.concatenate(
                    [jnp.where(low, both, nothing), jnp.where(low, nothing, both)], axis=0
                )
                inner = jnp.dot(
                    jnp.concatenate(weights, axis=1), apart, preferred_element_type=F32
                )
                head = chunk * CHUNK_HEADS + 2 * p
                skip = jnp.where(low[:1], skip_ref[0, head], skip_ref[0, head + 1])
                part = x_ref[:, at].astype(F32) + inner + skip * both.astype(F32)
                part_out[chunk, :, p * 128 : (p + 1) * 128] = part.astype(BF16)
        for q in range(RING):
            part_copy(q * CHUNKS + j).start()

    def spread_decay(j):
        cols = columns(cum_in, j)
        for q in range(RING):
            chunk = q * CHUNKS + j
            for p in range(PAIRS):
                lane_at = q * (HEADS // RING) + 2 * p
                spread = jnp.where(
                    low, cols[:, lane_at : lane_at + 1], cols[:, lane_at + 1 : lane_at + 2]
                )
                grown[:, pair_lanes(chunk, p)] = jnp.exp2(spread)

    def finish(j):
        for distance in (0, 1, 3, 2):
            q = (place + distance) % RING
            chunk = q * CHUNKS + j
            lanes = lanes_of(chunk)
            group = pl.ds(pl.multiple_of((chunk // GROUP_CHUNKS) * STATE, STATE), STATE)
            part_copy(chunk).wait_recv()
            back_copy(place, q, j).wait_recv()
            carried = jnp.dot(read_in[:, group], back_in[q, j], preferred_element_type=F32)
            out_ref[:, lanes] = (part_in[chunk].astype(F32) + grown[:, lanes] * carried).astype(
                BF16
            )

    def settle(j):
        for distance in range(1, RING):
            to = (place + distance) % RING
            sum_copy(to, place, j).wait_send()

        for to in range(RING):
            back_copy(to, place, j).wait_send()

        @pl.when(ctx < blocks - 1)
        def _():
            halo_copy(j).wait_send()

        @pl.when(passes_on)
        def _():
            state_copy(j, 2).wait_send()
            state_copy(j, 1).wait_send()

        @pl.when(jnp.logical_not(second))
        def _():
            front_copy(j).wait_send()

        for q in range(RING):
            part_copy(q * CHUNKS + j).wait_send()

    relay_lag = jnp.where(second, jnp.minimum(ODD + row, CHUNKS), EVEN)
    back_lag = jnp.where(second, jnp.maximum(relay_lag + LAG - row, CHUNKS), EVEN + LAG)
    finish_lag = back_lag + LATER

    def only(j, step):
        @pl.when((j >= 0) & (j < CHUNKS))
        def _():
            step(j)

    def pipeline(i, carry):
        @pl.when((i > 0) & (i < CHUNKS))
        def _():
            produce(i)

        @pl.when(i == 2)
        def _():
            for distance in range(1, RING):
                source = (place + distance) % RING
                end_copy(source, place).wait_send()
                end_copy(source, source).wait_recv()
            for copy in map_copies(0, 1):
                copy.wait()

            @pl.when(jnp.logical_not(second))
            def _():
                ends = [end_in[block, pl.ds(0, END_ROWS), :] for block in range(RING)]
                fade_out[...] = (ends[0] + ends[1]) + (ends[2] + ends[3])
                fade_copy().start()

            @pl.when(second)
            def _():
                fade_copy().wait_recv()

        only(i - relay_lag, relay)
        only(i - back_lag, hand_back)
        only(i, within)
        only(i - 2, spread_decay)
        only(i - finish_lag, settle)
        only(i - finish_lag, finish)
        return carry

    lax.fori_loop(0, CHUNKS + finish_lag, pipeline, 0)

    for distance in range(1, RING):
        head_copy((place + distance) % RING, place).wait_send()

    @pl.when(jnp.logical_not(second))
    def _():
        fade_copy().wait_send()


def shards(
    section_input, norm_gain, conv_weight, state_write, state_read, step_size, log_decay, skip_gain
):
    hbm = pl.BlockSpec(memory_space=pltpu.HBM)
    dma = pltpu.SemaphoreType.DMA
    chunks = WIDTH // LANES
    half = (RING, CHUNKS, STATE, LANES)
    halo = (CHUNKS, 2, 16, 128)
    handed = pl.pallas_call(
        mixing_kernel,
        out_shape=jax.ShapeDtypeStruct((SPAN, WIDTH), BF16),
        in_specs=[hbm] * 8,
        out_specs=pl.BlockSpec(memory_space=pltpu.VMEM),
        scratch_shapes=[
            pltpu.VMEM((SPAN, WIDTH), BF16),
            pltpu.VMEM((1, WIDTH), BF16),
            pltpu.VMEM((CONV, WIDTH), BF16),
            pltpu.VMEM((SPAN, GROUPS * STATE), BF16),
            pltpu.VMEM((SPAN, GROUPS * STATE), BF16),
            pltpu.VMEM((HEADS, SPAN), F32),
            pltpu.VMEM((HEADS, SPAN), F32),
            pltpu.SMEM((1, HEADS), F32),
            pltpu.VMEM((SPAN, 128), F32),
            pltpu.VMEM((RING * PAIRS, SPAN + 8, 128), F32),
            pltpu.VMEM((SPAN, WIDTH), BF16),
            pltpu.VMEM((SPAN, WIDTH), F32),
            pltpu.VMEM((GROUPS, SPAN, SPAN), F32),
            pltpu.VMEM((GROUPS, STATE, SPAN), BF16),
            pltpu.VMEM((HEADS, SPAN), F32),
            pltpu.VMEM((SPAN, HEADS), F32),
            pltpu.VMEM((HEADS + 8, SPAN), F32),
            pltpu.VMEM((SPAN, HEADS), F32),
            pltpu.VMEM(halo, BF16),
            pltpu.VMEM(halo, BF16),
            pltpu.VMEM((RING, END_ROWS + 8, 128), F32),
            pltpu.VMEM((RING, END_ROWS + 8, 128), F32),
            pltpu.VMEM(half, BF16),
            pltpu.VMEM(half, BF16),
            pltpu.VMEM(half[1:], BF16),
            pltpu.VMEM(half[1:], BF16),
            pltpu.VMEM(half[1:], BF16),
            pltpu.VMEM(half[1:], BF16),
            pltpu.VMEM((END_ROWS, 128), F32),
            pltpu.VMEM((END_ROWS + 8, 128), F32),
            pltpu.VMEM((RING, 16, LANES + STATE), BF16),
            pltpu.VMEM((RING, 16, LANES + STATE), BF16),
            pltpu.VMEM(half, BF16),
            pltpu.VMEM(half, BF16),
            pltpu.VMEM((chunks, SPAN, LANES), BF16),
            pltpu.VMEM((chunks, SPAN, LANES), BF16),
            pltpu.VMEM((SPAN, GROUPS * STATE), BF16),
            pltpu.VMEM((SPAN, HEADS), F32),
            dma((9,)),
            dma((2, CHUNKS)),
            dma((2, RING)),
            dma((2, RING)),
            dma((2, RING, CHUNKS)),
            dma((3, CHUNKS)),
            dma((2, CHUNKS)),
            dma((2,)),
            dma((2, RING, CHUNKS)),
            dma((2, chunks)),
            dma((2, 2)),
        ],
        compiler_params=pltpu.CompilerParams(
            collective_id=0, has_side_effects=True, vmem_limit_bytes=48 << 20
        ),
    )(
        *(
            pltpu.with_memory_space_constraint(operand, pltpu.HBM)
            for operand in (
                section_input[0],
                norm_gain,
                conv_weight[0],
                state_write[0],
                state_read[0],
                step_size[0],
                log_decay[0],
                skip_gain,
            )
        )
    )
    return handed[None]


def solution(mesh):
    in_specs = (
        P("section", "ctx", None),
        P("section", None),
        P("section", None, None),
        P("section", "ctx", None),
        P("section", "ctx", None),
        P("section", None, "ctx"),
        P("section", None, "ctx"),
        P("section", None),
    )
    out_specs = P("section", "ctx", None)
    return jax.shard_map(shards, mesh=mesh, in_specs=in_specs, out_specs=out_specs, check_vma=False)
```

```python
import jax
import jax.numpy as jnp
from jax import lax
from jax.experimental import pallas as pl
from jax.experimental.pallas import tpu as pltpu
from jax.sharding import PartitionSpec as P

HEADS = 128
HEAD_DIM = 64
STATE = 128
GROUPS = 8
CONV = 4
SPAN = 128
WIDTH = HEADS * HEAD_DIM
RING = 4
LANES = 256
PAIRS = LANES // 128
CHUNK_HEADS = LANES // HEAD_DIM
CHUNKS = WIDTH // RING // LANES
GROUP_CHUNKS = WIDTH // GROUPS // LANES
LATER = 3
EVEN = 3
ODD = 3
LAG = 4
END_ROWS = CHUNKS * PAIRS
LOG2E = 1.4426950408889634
F32 = jnp.float32
BF16 = jnp.bfloat16


def mixing_kernel(
    x_hbm, gain_hbm, taps_hbm, write_hbm, read_hbm, step_hbm, decay_hbm, skip_hbm,
    out_ref,
    x_ref, gain_ref, taps_ref, write_ref, read_ref, step_ref, decay_ref, skip_ref,
    scale_buf, padded, mixed, grown, scores, write_t, cum_rows, cum_cols, shift_rows, shift_cols,
    halo_out, halo_in, end_out, end_in, sum_out, sum_in, state_in, state_out,
    front_out, front_in, fade_out, fade_in, head_out, head_in,
    back_out, back_in, part_out, part_in, read_in, cum_in,
    fetch_sems, halo_sems, end_sems, head_sems, sum_sems, state_sems, front_sems, fade_sems, back_sems, part_sems, map_sems,
):
    sections, blocks = lax.axis_size("section"), lax.axis_size("ctx")
    rows = blocks // RING
    section, ctx = lax.axis_index("section"), lax.axis_index("ctx")
    row, place = ctx // RING, ctx % RING
    second = row % 2 == 1
    passes_on = second & (row < rows - 1)

    def at_ctx(index):
        return {"section": section, "ctx": index}

    def at_place(index):
        return at_ctx(row * RING + index)

    before_ctx, after_ctx = (ctx + blocks - 1) % blocks, (ctx + 1) % blocks
    before_section, after_section = (section + sections - 1) % sections, (section + 1) % sections

    def next_layer(index):
        return {"section": after_section, "ctx": row * RING + index}

    barrier = pltpu.get_barrier_semaphore()
    for index in range(RING):
        holder = {"section": before_section, "ctx": row * RING + index}
        pl.semaphore_signal(barrier, 1, device_id=holder)
    for distance in range(1, RING):
        pl.semaphore_signal(barrier, 1, device_id=at_place((place + distance) % RING))

    @pl.when(ctx > 0)
    def _():
        pl.semaphore_signal(barrier, 1, device_id=at_ctx(before_ctx))

    @pl.when(row > 0)
    def _():
        pl.semaphore_signal(barrier, 1, device_id=at_ctx(ctx - RING))

    @pl.when(second & (row > 1))
    def _():
        pl.semaphore_signal(barrier, 1, device_id=at_ctx(ctx - 2 * RING))

    late = SPAN - 16
    fetches = [
        pltpu.make_async_copy(source, target, fetch_sems.at[i])
        for i, (source, target) in enumerate(
            [
                (x_hbm.at[pl.ds(late, 16)], x_ref.at[pl.ds(late, 16)]),
                (gain_hbm, gain_ref),
                (decay_hbm, decay_ref),
                (step_hbm, step_ref),
                (x_hbm.at[pl.ds(0, late)], x_ref.at[pl.ds(0, late)]),
                (taps_hbm, taps_ref),
                (write_hbm, write_ref),
                (read_hbm, read_ref),
                (skip_hbm, skip_ref),
            ]
        )
    ]
    for fetch in fetches:
        fetch.start()

    def halo_copy(j):
        return pltpu.make_async_remote_copy(
            src_ref=halo_out.at[j], dst_ref=halo_in.at[j],
            send_sem=halo_sems.at[0, j], recv_sem=halo_sems.at[1, j],
            device_id=at_ctx(after_ctx),
        )

    def end_copy(to, slot):
        return pltpu.make_async_remote_copy(
            src_ref=end_out.at[to, pl.ds(0, END_ROWS)], dst_ref=end_in.at[slot, pl.ds(0, END_ROWS)],
            send_sem=end_sems.at[0, to], recv_sem=end_sems.at[1, slot], device_id=at_place(to),
        )

    def sum_copy(to, slot, j):
        return pltpu.make_async_remote_copy(
            src_ref=sum_out.at[to, j], dst_ref=sum_in.at[slot, j],
            send_sem=sum_sems.at[0, to, j], recv_sem=sum_sems.at[1, slot, j],
            device_id=at_place(to),
        )

    def head_copy(to, slot):
        return pltpu.make_async_remote_copy(
            src_ref=head_out.at[to], dst_ref=head_in.at[slot],
            send_sem=head_sems.at[0, to], recv_sem=head_sems.at[1, slot], device_id=at_place(to),
        )

    def state_copy(j, hops):
        return pltpu.make_async_remote_copy(
            src_ref=state_out.at[j], dst_ref=state_in.at[j],
            send_sem=state_sems.at[hops, j], recv_sem=state_sems.at[0, j],
            device_id=at_ctx((ctx + hops * RING) % blocks),
        )

    def front_copy(j):
        return pltpu.make_async_remote_copy(
            src_ref=front_out.at[j], dst_ref=front_in.at[j],
            send_sem=front_sems.at[0, j], recv_sem=front_sems.at[1, j],
            device_id=at_ctx((ctx + RING) % blocks),
        )

    def fade_copy():
        return pltpu.make_async_remote_copy(
            src_ref=fade_out, dst_ref=fade_in.at[pl.ds(0, END_ROWS)], send_sem=fade_sems.at[0], recv_sem=fade_sems.at[1],
            device_id=at_ctx((ctx + RING) % blocks),
        )

    def back_copy(to, slot, j):
        return pltpu.make_async_remote_copy(
            src_ref=back_out.at[to, j], dst_ref=back_in.at[slot, j],
            send_sem=back_sems.at[0, to, j], recv_sem=back_sems.at[1, slot, j],
            device_id=next_layer(to),
        )

    def lanes_of(chunk):
        return pl.ds(pl.multiple_of(chunk * LANES, LANES), LANES)

    def part_copy(chunk):
        return pltpu.make_async_remote_copy(
            src_ref=part_out.at[chunk], dst_ref=part_in.at[chunk],
            send_sem=part_sems.at[0, chunk], recv_sem=part_sems.at[1, chunk],
            device_id=next_layer(place),
        )

    def map_copies(*which):
        return [
            pltpu.make_async_remote_copy(
                src_ref=source, dst_ref=target,
                send_sem=map_sems.at[0, i], recv_sem=map_sems.at[1, i],
                device_id=next_layer(place),
            )
            for i, (source, target) in enumerate([(cum_cols, cum_in), (read_ref, read_in)])
            if i in which
        ]

    def square_sum(first, count):
        def add(i, acc):
            part = x_ref[pl.ds(first, count), pl.ds(pl.multiple_of(i * 1024, 1024), 1024)]
            for k in range(8):
                piece = part[:, k * 128 : (k + 1) * 128].astype(F32)
                acc = acc + piece * piece
            return acc

        acc = lax.fori_loop(0, WIDTH // 1024, add, jnp.zeros((count, 128), F32))
        mean = jnp.sum(acc, axis=-1, keepdims=True) * (1.0 / WIDTH)
        return jnp.broadcast_to(lax.rsqrt(mean + 1e-05), (count, 128))

    fetches[0].wait()
    fetches[1].wait()
    tail_scale = square_sum(late, 16)
    for j in range(CHUNKS):
        for half in range(2):
            pieces = []
            for part in range(2 * PAIRS):
                q, p = 2 * half + part // PAIRS, part % PAIRS
                first = (q * CHUNKS + j) * LANES + p * 128
                span = slice(first, first + 128)
                normed = (x_ref[late:SPAN, span].astype(F32) * tail_scale) * gain_ref[
                    :, span
                ].astype(F32)
                pieces.append(normed[12:16, :])
            halo_out[j, half] = jnp.concatenate(pieces, axis=0).astype(BF16)

    token = lax.broadcasted_iota(jnp.int32, (SPAN, SPAN), 0)
    lane = lax.broadcasted_iota(jnp.int32, (SPAN, SPAN), 1)
    low = lane < HEAD_DIM
    causal = token >= lane
    upper = jnp.where(token <= lane, 1.0, 0.0).astype(F32)
    fetches[2].wait()
    cumul = lax.dot_general(
        decay_ref[...], upper, (((1,), (0,)), ((), ())),
        precision=lax.Precision.HIGHEST, preferred_element_type=F32,
    ) * LOG2E
    cum_rows[...] = cumul
    even, odd = (
        jnp.broadcast_to(cum_rows[pl.ds(first, HEADS // 2, stride=2), :][:, SPAN - 1 :], (HEADS // 2, 128))
        for first in range(2)
    )
    ends = jnp.where(low[: HEADS // 2], even, odd)
    end_out[:, pl.ds(0, END_ROWS), :] = ends.reshape(RING, END_ROWS, 128)
    end_in[place, pl.ds(0, END_ROWS), :] = end_out[place, pl.ds(0, END_ROWS), :]
    cum_cols[...] = cumul.T
    fetches[3].wait()
    shift = cumul - jnp.log2(step_ref[...])
    shift_rows[pl.ds(0, HEADS), :] = shift
    shift_cols[...] = shift.T

    fetches[4].wait()
    scale = square_sum(0, SPAN)
    for fetch in fetches[5:]:
        fetch.wait()

    for g in range(GROUPS):
        writes = write_ref[:, g * STATE : (g + 1) * STATE]
        write_t[g] = writes.astype(F32).T.astype(BF16)

    def columns(ref, j):
        return pltpu.roll(ref[...], (HEADS - j * CHUNK_HEADS) % HEADS, 1)

    def pair_lanes(chunk, p):
        return pl.ds(pl.multiple_of(chunk * LANES + p * 128, 128), 128)

    scale_buf[...] = scale

    def norm_chunk(j):
        for q in range(RING):
            for p in range(PAIRS):
                at = pair_lanes(q * CHUNKS + j, p)
                normed = (x_ref[:, at].astype(F32) * scale_buf[...]) * gain_ref[:, at].astype(F32)
                padded[q * PAIRS + p, 8:, :] = normed.astype(BF16).astype(F32)

    def take_halo(j):
        @pl.when(ctx > 0)
        def _():
            halo_copy(j).wait_recv()

        before = [halo_in[j, half].astype(F32) for half in range(2)]
        for q in range(RING):
            for p in range(PAIRS):
                first = 4 * (q % 2 * PAIRS + p)
                padded[q * PAIRS + p, 4:8, :] = before[q // 2][first : first + 4, :]

    def mix(j, q, p, count, cols):
        at = pair_lanes(q * CHUNKS + j, p)
        buffer = padded.at[q * PAIRS + p]
        taps = taps_ref[:, at].astype(F32)
        acc = taps[0:1, :] * buffer[8 - (CONV - 1) : 8 - (CONV - 1) + count, :]
        for k in range(1, CONV):
            first = 8 - (CONV - 1) + k
            acc = acc + taps[k : k + 1, :] * buffer[first : first + count, :]
        acc = acc * (0.5 + 0.5 * jnp.tanh(0.5 * acc))
        value = acc.astype(BF16)
        mixed[pl.ds(0, count), at] = value
        head = q * (HEADS // RING) + 2 * p
        spread = jnp.where(
            low[:count], cols[:count, head : head + 1], cols[:count, head + 1 : head + 2]
        )
        end = end_out[q, pl.ds(j * PAIRS + p, 1), :]
        return value.astype(F32) * jnp.exp2(end - spread)

    def send_sums(j):
        for distance in (2, 1, 3):
            sum_copy((place + distance) % RING, place, j).start()
        sum_in[place, j] = sum_out[place, j]

    def summarize(j, kept):
        cols = columns(shift_cols, j)
        for q in range(RING):
            parts = [kept(mix(j, q, p, SPAN, cols)).astype(BF16) for p in range(PAIRS)]
            sum_out[q, j] = jnp.dot(
                write_t[(q * CHUNKS + j) // GROUP_CHUNKS],
                jnp.concatenate(parts, axis=1),
                preferred_element_type=F32,
            ).astype(BF16)
        send_sums(j)

    def produce(j):
        norm_chunk(j)
        take_halo(j)
        summarize(j, lambda scaled: scaled)

    def produce_first():
        for q in range(RING * PAIRS):
            padded[q, 0:8, :] = jnp.zeros((8, 128), F32)
        norm_chunk(0)
        summarize(0, lambda scaled: jnp.where(token >= CONV - 1, scaled, 0.0))

    def complete_first():
        take_halo(0)
        cols = columns(shift_cols, 0)
        for q in range(RING):
            parts = [
                jnp.where(token[:16] < CONV - 1, mix(0, q, p, 16, cols), 0.0).astype(BF16)
                for p in range(PAIRS)
            ]
            group = q * CHUNKS // GROUP_CHUNKS * STATE
            parts.append(write_ref[0:16, group : group + STATE])
            head_out[q] = jnp.concatenate(parts, axis=1)
        for distance in range(1, RING):
            head_copy((place + distance) % RING, place).start()
        head_in[place] = head_out[place]

    def add_first():
        for distance in range(1, RING):
            source = (place + distance) % RING
            head_copy(source, source).wait_recv()
            sum_copy(source, source, 0).wait_recv()
        for source in range(RING):
            maps = head_in[source, :, LANES:].astype(F32).T.astype(BF16)
            added = jnp.dot(maps, head_in[source, :, :LANES], preferred_element_type=F32)
            sum_in[source, 0] = (sum_in[source, 0].astype(F32) + added).astype(BF16)

    pl.semaphore_wait(
        barrier,
        2 * RING - 1
        + jnp.where(ctx < blocks - 1, 1, 0)
        + jnp.where(second, jnp.where(row < rows - 1, 2, 0), 1),
    )

    @pl.when(ctx < blocks - 1)
    def _():
        for j in range(CHUNKS):
            halo_copy(j).start()

    @pl.when(ctx == 0)
    def _():
        halo_in[...] = jnp.zeros_like(halo_in)

    for distance in range(1, RING):
        to = (place + distance) % RING
        end_copy(to, place).start()
    for copy in map_copies(0, 1):
        copy.start()

    produce_first()
    for g in range(GROUPS):
        span = slice(g * STATE, (g + 1) * STATE)
        scores[g] = lax.dot_general(
            read_ref[:, span], write_ref[:, span], (((1,), (1,)), ((), ())),
            preferred_element_type=F32,
        )
    complete_first()

    @pl.when(row < 2)
    def _():
        state_in[...] = jnp.zeros_like(state_in)

    @pl.when(jnp.logical_not(second))
    def _():
        front_in[...] = jnp.zeros_like(front_in)
        fade_in[...] = jnp.zeros_like(fade_in)

    def spread_row(ref, j):
        return jnp.concatenate(
            [jnp.exp2(ref[pl.ds(j * PAIRS + p, 1), :]) for p in range(PAIRS)], axis=1
        )

    def factor(source, j):
        return spread_row(end_in.at[source], j)

    def relay(j):
        @pl.when(j == 0)
        def _():
            add_first()

        @pl.when(j > 0)
        def _():
            for distance in range(1, RING):
                source = (place + distance) % RING
                sum_copy(source, source, j).wait_recv()

        whole = factor(0, j)
        summed = sum_in[0, j].astype(F32)
        for block in range(1, RING):
            one = factor(block, j)
            whole = whole * one
            summed = summed * one + sum_in[block, j].astype(F32)

        @pl.when(jnp.logical_not(second))
        def _():
            front_out[j] = summed.astype(BF16)
            front_copy(j).start()

        @pl.when(second)
        def _():
            front_copy(j).wait_recv()

            @pl.when(row > 1)
            def _():
                state_copy(j, 1).wait_recv()

        @pl.when(passes_on)
        def _():
            state_out[j] = (entering(j) * whole + summed).astype(BF16)
            state_copy(j, 2).start()
            state_copy(j, 1).start()

    def entering(j):
        return state_in[j].astype(F32) * spread_row(fade_in, j) + front_in[j].astype(F32)

    def hand_back(j):
        @pl.when(jnp.logical_not(second) & (row > 0))
        def _():
            state_copy(j, 1).wait_recv()

        state = entering(j)
        back_out[0, j] = state.astype(BF16)
        for block in range(1, RING):
            state = state * factor(block - 1, j) + sum_in[block - 1, j].astype(F32)
            back_out[block, j] = state.astype(BF16)
        for distance in (2, 1, 3, 0):
            back_copy((place + distance) % RING, place, j).start()

    def within(j):
        cols = columns(cum_cols, j)
        for q in range(RING):
            chunk = q * CHUNKS + j
            score = scores[chunk // GROUP_CHUNKS]
            for p in range(PAIRS):
                at = pair_lanes(chunk, p)
                weights = []
                for k in range(2):
                    lane_at = q * (HEADS // RING) + 2 * p + k
                    decay = jnp.broadcast_to(cols[:, lane_at : lane_at + 1], (SPAN, SPAN))
                    row_at = pl.ds(chunk * CHUNK_HEADS + 2 * p + k, 1)
                    weight = score * jnp.exp2(decay - shift_rows[row_at, :])
                    weights.append(jnp.where(causal, weight, 0.0).astype(BF16))
                both = mixed[:, at]
                nothing = jnp.zeros_like(both)
                apart = jnp.concatenate(
                    [jnp.where(low, both, nothing), jnp.where(low, nothing, both)], axis=0
                )
                inner = jnp.dot(
                    jnp.concatenate(weights, axis=1), apart, preferred_element_type=F32
                )
                head = chunk * CHUNK_HEADS + 2 * p
                skip = jnp.where(low[:1], skip_ref[0, head], skip_ref[0, head + 1])
                part = x_ref[:, at].astype(F32) + inner + skip * both.astype(F32)
                part_out[chunk, :, p * 128 : (p + 1) * 128] = part.astype(BF16)
        for q in range(RING):
            part_copy(q * CHUNKS + j).start()

    def spread_decay(j):
        cols = columns(cum_in, j)
        for q in range(RING):
            chunk = q * CHUNKS + j
            for p in range(PAIRS):
                lane_at = q * (HEADS // RING) + 2 * p
                spread = jnp.where(
                    low, cols[:, lane_at : lane_at + 1], cols[:, lane_at + 1 : lane_at + 2]
                )
                grown[:, pair_lanes(chunk, p)] = jnp.exp2(spread)

    def finish(j):
        for distance in (0, 1, 3, 2):
            q = (place + distance) % RING
            chunk = q * CHUNKS + j
            lanes = lanes_of(chunk)
            group = pl.ds(pl.multiple_of((chunk // GROUP_CHUNKS) * STATE, STATE), STATE)
            part_copy(chunk).wait_recv()
            back_copy(place, q, j).wait_recv()
            carried = jnp.dot(read_in[:, group], back_in[q, j], preferred_element_type=F32)
            out_ref[:, lanes] = (part_in[chunk].astype(F32) + grown[:, lanes] * carried).astype(
                BF16
            )

    def settle(j):
        for distance in range(1, RING):
            to = (place + distance) % RING
            sum_copy(to, place, j).wait_send()

        for to in range(RING):
            back_copy(to, place, j).wait_send()

        @pl.when(ctx < blocks - 1)
        def _():
            halo_copy(j).wait_send()

        @pl.when(passes_on)
        def _():
            state_copy(j, 2).wait_send()
            state_copy(j, 1).wait_send()

        @pl.when(jnp.logical_not(second))
        def _():
            front_copy(j).wait_send()

        for q in range(RING):
            part_copy(q * CHUNKS + j).wait_send()

    relay_lag = jnp.where(second, jnp.minimum(ODD + row, CHUNKS), EVEN)
    back_lag = jnp.where(second, jnp.maximum(relay_lag + LAG - row, CHUNKS), EVEN + LAG)
    finish_lag = back_lag + LATER

    def only(j, step):
        @pl.when((j >= 0) & (j < CHUNKS))
        def _():
            step(j)

    def pipeline(i, carry):
        @pl.when((i > 0) & (i < CHUNKS))
        def _():
            produce(i)

        @pl.when(i == 2)
        def _():
            for distance in range(1, RING):
                source = (place + distance) % RING
                end_copy(source, place).wait_send()
                end_copy(source, source).wait_recv()
            for copy in map_copies(0, 1):
                copy.wait()

            @pl.when(jnp.logical_not(second))
            def _():
                ends = [end_in[block, pl.ds(0, END_ROWS), :] for block in range(RING)]
                fade_out[...] = (ends[0] + ends[1]) + (ends[2] + ends[3])
                fade_copy().start()

            @pl.when(second)
            def _():
                fade_copy().wait_recv()

        only(i - relay_lag, relay)
        only(i - back_lag, hand_back)
        only(i, within)
        only(i - 2, spread_decay)
        only(i - finish_lag, settle)
        only(i - finish_lag, finish)
        return carry

    lax.fori_loop(0, CHUNKS + finish_lag, pipeline, 0)

    for distance in range(1, RING):
        head_copy((place + distance) % RING, place).wait_send()

    @pl.when(jnp.logical_not(second))
    def _():
        fade_copy().wait_send()


def shards(
    section_input, norm_gain, conv_weight, state_write, state_read, step_size, log_decay, skip_gain
):
    hbm = pl.BlockSpec(memory_space=pltpu.HBM)
    dma = pltpu.SemaphoreType.DMA
    chunks = WIDTH // LANES
    half = (RING, CHUNKS, STATE, LANES)
    halo = (CHUNKS, 2, 16, 128)
    handed = pl.pallas_call(
        mixing_kernel,
        out_shape=jax.ShapeDtypeStruct((SPAN, WIDTH), BF16),
        in_specs=[hbm] * 8,
        out_specs=pl.BlockSpec(memory_space=pltpu.VMEM),
        scratch_shapes=[
            pltpu.VMEM((SPAN, WIDTH), BF16),
            pltpu.VMEM((1, WIDTH), BF16),
            pltpu.VMEM((CONV, WIDTH), BF16),
            pltpu.VMEM((SPAN, GROUPS * STATE), BF16),
            pltpu.VMEM((SPAN, GROUPS * STATE), BF16),
            pltpu.VMEM((HEADS, SPAN), F32),
            pltpu.VMEM((HEADS, SPAN), F32),
            pltpu.SMEM((1, HEADS), F32),
            pltpu.VMEM((SPAN, 128), F32),
            pltpu.VMEM((RING * PAIRS, SPAN + 8, 128), F32),
            pltpu.VMEM((SPAN, WIDTH), BF16),
            pltpu.VMEM((SPAN, WIDTH), F32),
            pltpu.VMEM((GROUPS, SPAN, SPAN), F32),
            pltpu.VMEM((GROUPS, STATE, SPAN), BF16),
            pltpu.VMEM((HEADS, SPAN), F32),
            pltpu.VMEM((SPAN, HEADS), F32),
            pltpu.VMEM((HEADS + 8, SPAN), F32),
            pltpu.VMEM((SPAN, HEADS), F32),
            pltpu.VMEM(halo, BF16),
            pltpu.VMEM(halo, BF16),
            pltpu.VMEM((RING, END_ROWS + 8, 128), F32),
            pltpu.VMEM((RING, END_ROWS + 8, 128), F32),
            pltpu.VMEM(half, BF16),
            pltpu.VMEM(half, BF16),
            pltpu.VMEM(half[1:], BF16),
            pltpu.VMEM(half[1:], BF16),
            pltpu.VMEM(half[1:], BF16),
            pltpu.VMEM(half[1:], BF16),
            pltpu.VMEM((END_ROWS, 128), F32),
            pltpu.VMEM((END_ROWS + 8, 128), F32),
            pltpu.VMEM((RING, 16, LANES + STATE), BF16),
            pltpu.VMEM((RING, 16, LANES + STATE), BF16),
            pltpu.VMEM(half, BF16),
            pltpu.VMEM(half, BF16),
            pltpu.VMEM((chunks, SPAN, LANES), BF16),
            pltpu.VMEM((chunks, SPAN, LANES), BF16),
            pltpu.VMEM((SPAN, GROUPS * STATE), BF16),
            pltpu.VMEM((SPAN, HEADS), F32),
            dma((9,)),
            dma((2, CHUNKS)),
            dma((2, RING)),
            dma((2, RING)),
            dma((2, RING, CHUNKS)),
            dma((3, CHUNKS)),
            dma((2, CHUNKS)),
            dma((2,)),
            dma((2, RING, CHUNKS)),
            dma((2, chunks)),
            dma((2, 2)),
        ],
        compiler_params=pltpu.CompilerParams(
            collective_id=0, has_side_effects=True, vmem_limit_bytes=48 << 20
        ),
    )(
        *(
            pltpu.with_memory_space_constraint(operand, pltpu.HBM)
            for operand in (
                section_input[0],
                norm_gain,
                conv_weight[0],
                state_write[0],
                state_read[0],
                step_size[0],
                log_decay[0],
                skip_gain,
            )
        )
    )
    return handed[None]


def solution(mesh):
    in_specs = (
        P("section", "ctx", None),
        P("section", None),
        P("section", None, None),
        P("section", "ctx", None),
        P("section", "ctx", None),
        P("section", None, "ctx"),
        P("section", None, "ctx"),
        P("section", None),
    )
    out_specs = P("section", "ctx", None)
    return jax.shard_map(shards, mesh=mesh, in_specs=in_specs, out_specs=out_specs, check_vma=False)
```
